128 devices in a mesh: row: 32 (over z_lo, y, x), col: 4 (over z_hi, core).
Axes of the slice: x: 4, y: 4, z: 4 (z_hi: 2, z_lo: 2; z = z_hi * 2 + z_lo), core: 2. Of those that a mesh axis runs over, the one named last changes fastest.
Arguments:
- panel_tiles: float32 [65536, 1024], P('row', 'col'), may hold values from -48 to 48
- left_u: bfloat16 [65536, 6144], P('row', 'col'), may hold values from -8 to 8
- earlier_right_factors: bfloat16 [65536, 6144], P('row', 'col'), may hold values from -0.25 to 0.25
- tile_global_index: int32 [64], replicated, may hold values from 0 to 63, as said below
Outputs:
- panel_factor: float32 [65536, 1024], P('row', 'col')
The draws below stay inside these ranges and needn't reach their ends.
Inputs may be any that keep to these rules, and one draw needn't show every extreme that they name: `tile_global_index`: A permutation; slot pivot, the one numbered 0, holds the diagonal tile.
All inputs are finite; a program needn't handle non-finite values.
Results may differ from the reference program's by a relative error of at most 0.00053.
Values may be sent and summed in bfloat16 or wider, within the bound.
No kernel may reach another device: no remote copies, remote signals or barrier semaphores. Data moves between devices by JAX's collectives and lax.ppermute only.
A program may use at most 128 MiB of HBM per device.

```python
import math
import jax
import jax.numpy as jnp
from jax import lax

TILE = 1024
RANK = 256
TILES = 64
COLS = 24


kernel_height = 30.0


nugget_level = 16.0


factor_bound = 0.25


def pivot_draw(key):
    ordering = jax.random.permutation(jax.random.fold_in(key, 11), TILES).astype(jnp.int32)
    pivot_position = jnp.sum(jnp.where(ordering == 0, jnp.arange(TILES, dtype=jnp.int32), 0)).astype(jnp.int32)
    return (ordering, pivot_position)


def update_scale():
    aspect_ratio = TILE / (COLS * RANK)
    edge_factor = (1.0 + math.sqrt(aspect_ratio)) ** 2 * (1.0 + 0.5 * RANK / TILE)
    margin_factor = 1.05 + 1.5 / math.sqrt(TILE)
    return math.sqrt(nugget_level / (edge_factor * margin_factor * COLS * RANK))


def draw_tile_global_index(key, part):
    ordering, pivot_position = pivot_draw(key)
    return ordering


def draw_panel_tiles(key, part):
    ordering, pivot_position = pivot_draw(key)
    background = jnp.clip(jax.random.normal(jax.random.fold_in(key, 21), (TILES * TILE, TILE), jnp.float32), -6.0, 6.0) * 0.5
    length_scale = 0.15
    points = jax.random.uniform(jax.random.fold_in(key, 24), (TILE, 2), jnp.float32)
    offsets = points[:, None, :] - points[None, :, :]
    distance = jnp.sqrt(jnp.sum(offsets * offsets, axis=2))
    pivot_block = kernel_height * jnp.exp(-distance / length_scale) + nugget_level * jnp.eye(TILE, dtype=jnp.float32)
    start_row = (pivot_position * TILE).astype(jnp.int32)
    result = lax.dynamic_update_slice(background, pivot_block, (start_row, jnp.int32(0)))
    return result.astype(jnp.float32)


def draw_left_u(key, part):
    ordering, pivot_position = pivot_draw(key)
    background = jnp.clip(jax.random.normal(jax.random.fold_in(key, 31), (TILES * TILE, COLS * RANK), jnp.float32), -6.0, 6.0) * 0.3
    pivot_rows = jnp.clip(jax.random.normal(jax.random.fold_in(key, 32), (TILE, COLS * RANK), jnp.float32), -6.0, 6.0) * update_scale()
    start_row = (pivot_position * TILE).astype(jnp.int32)
    result = lax.dynamic_update_slice(background, pivot_rows, (start_row, jnp.int32(0)))
    return result.astype(jnp.bfloat16)


def draw_earlier_right_factors(key, part):
    normal_draw = jnp.clip(jax.random.normal(jax.random.fold_in(key, 41), (TILES * TILE, COLS * RANK), jnp.float32), -6.0, 6.0)
    scaled = jnp.clip(normal_draw * (1.0 / math.sqrt(TILE)), -factor_bound, factor_bound)
    return scaled.astype(jnp.bfloat16)


def setup_inputs(seed: int = 0) -> dict:
    seeds = jax.random.split(jax.random.key(seed), 5)
    return {
        "panel_tiles": draw_panel_tiles(jax.random.fold_in(seeds[4], 71), 0),
        "left_u": draw_left_u(jax.random.fold_in(seeds[4], 71), 0),
        "earlier_right_factors": draw_earlier_right_factors(jax.random.fold_in(seeds[4], 71), 0),
        "tile_global_index": draw_tile_global_index(jax.random.fold_in(seeds[4], 71), 0),
    }


def reference(panel_tiles, left_u, earlier_right_factors, tile_global_index):
    pivot_position = jnp.sum(jnp.where(tile_global_index == 0, jnp.arange(TILES, dtype=jnp.int32), 0)).astype(jnp.int32)
    first_row = (pivot_position * TILE).astype(jnp.int32)
    pivot_left = lax.dynamic_slice_in_dim(left_u, first_row, TILE, 0)
    pivot_right = lax.dynamic_slice_in_dim(earlier_right_factors, first_row, TILE, 0)
    pivot_triple = pivot_right.astype(jnp.float32).reshape(TILE, COLS, RANK)

    def tile_update(factors):
        u_rows, v_rows = factors
        inner_small = jnp.einsum('bjr,bjs->jrs', v_rows.astype(jnp.float32).reshape(TILE, COLS, RANK), pivot_triple).astype(jnp.bfloat16)
        left_small = jnp.einsum('bjr,jrs->bjs', u_rows.astype(jnp.float32).reshape(TILE, COLS, RANK), inner_small.astype(jnp.float32)).astype(jnp.bfloat16)
        return jnp.dot(left_small.reshape(TILE, COLS * RANK).astype(jnp.float32), pivot_left.T.astype(jnp.float32), preferred_element_type=jnp.float32)
    update_terms = lax.map(tile_update, (left_u.reshape(TILES, TILE, COLS * RANK), earlier_right_factors.reshape(TILES, TILE, COLS * RANK)))
    updated_tiles = panel_tiles.reshape(TILES, TILE, TILE) - update_terms
    diagonal = lax.dynamic_index_in_dim(updated_tiles, pivot_position, 0, keepdims=False)
    cholesky_factor = jnp.linalg.cholesky(diagonal)
    identity = jnp.eye(TILE, dtype=jnp.float32)
    inverted_factor = lax.linalg.triangular_solve(cholesky_factor, identity, left_side=True, lower=True)
    solved_rows = jnp.einsum('fvk,ik->fvi', updated_tiles, inverted_factor, precision=lax.Precision.HIGHEST)
    chosen = (jnp.arange(TILES, dtype=jnp.int32) == pivot_position)[:, None, None]
    result = jnp.where(chosen, cholesky_factor[None, :, :], solved_rows)
    return result.reshape(TILES * TILE, TILE)
```

```python
import jax
import jax.numpy as jnp
from jax import lax
from jax.sharding import Mesh
from jax.sharding import PartitionSpec as P

TILE = 1024
RANK = 256
TILE_DEV = 2
COL_DEV = 6
BLOCK = 256
ROW = ("zl", "y", "x")
COL = ("zh", "core")
LOWER = ((0, 0), (1, 1), (2, 2), (1, 0), (2, 0), (3, 3), (2, 1), (3, 2), (3, 1), (3, 0))


def shift(value, axis, step):
    devices = lax.axis_size(axis)
    return lax.ppermute(value, axis, [(i, (i + step) % devices) for i in range(devices)])


def scatter(value, axis, away):
    quarter = value.shape[0] // 4
    parts = [value[k * quarter : (k + 1) * quarter] for k in range(4)]
    got = [parts[0]] + [shift(parts[k], axis, k) for k in (1, 2, 3)]
    return lax.select_n(away, *got)


def gather(piece, axis, away):
    quarter = piece.shape[0]
    got = [piece] + [shift(piece, axis, k) for k in (1, 2, 3)]
    whole = jnp.zeros((4 * quarter, *piece.shape[1:]), piece.dtype)
    for k in range(4):
        whole = lax.dynamic_update_slice_in_dim(whole, got[k], (away - k) % 4 * quarter, 0)
    return whole


def from_root(value, first, second, away):
    piece = scatter(value, first, away[first])
    piece = scatter(piece, second, away[second])
    piece = jnp.where(away["zl"] == 0, piece, shift(piece, "zl", 1))
    piece = gather(piece, second, away[second])
    return gather(piece, first, away[first])


def low_rank(left, right, pivot_right):
    rows = left.shape[0] // TILE
    left = left.reshape(rows, TILE, COL_DEV, RANK)
    right = right.reshape(rows, TILE, COL_DEV, RANK)
    pivot_right = pivot_right.reshape(TILE, COL_DEV, RANK)
    inner = jnp.einsum(
        "tbjr,bjs->tjrs", right, pivot_right, preferred_element_type=jnp.float32
    ).astype(jnp.bfloat16)
    product = jnp.einsum(
        "tbjr,tjrs->tbjs", left, inner, preferred_element_type=jnp.float32
    ).astype(jnp.bfloat16)
    return product.reshape(rows * TILE, COL_DEV * RANK)


def times_transposed(a, b):
    return lax.dot_general(a, b, (((1,), (1,)), ((), ())), preferred_element_type=jnp.float32)


def local(panel_tiles, left_u, earlier_right_factors, tile_global_index):
    tile_count = tile_global_index.shape[0]
    pivot_position = jnp.sum(
        jnp.where(tile_global_index == 0, jnp.arange(tile_count, dtype=jnp.int32), 0)
    )
    owner = pivot_position // TILE_DEV
    slot = pivot_position % TILE_DEV
    away = {
        "x": (lax.axis_index("x") - owner % 4) % 4,
        "y": (lax.axis_index("y") - owner // 4 % 4) % 4,
        "zl": (lax.axis_index("zl") - owner // 16) % 2,
    }
    zh, core = lax.axis_index("zh"), lax.axis_index("core")
    my_col = lax.axis_index(COL)

    own_left = lax.dynamic_slice_in_dim(left_u, slot * TILE, TILE, 0)
    own_right = lax.dynamic_slice_in_dim(earlier_right_factors, slot * TILE, TILE, 0)
    own_panel = lax.dynamic_slice_in_dim(panel_tiles, slot * TILE, TILE, 0)
    pivot_right = from_root(own_right, "x", "y", away)
    pivot_left = from_root(own_left, "y", "x", away)

    term = -times_transposed(low_rank(own_left, own_right, own_right), own_left)
    mine = lax.dynamic_slice_in_dim(term, my_col * BLOCK, BLOCK, 1) + own_panel
    term = lax.dynamic_update_slice_in_dim(term, mine, my_col * BLOCK, 1)
    grid = term.reshape(4, BLOCK, 4, BLOCK)
    lower = jnp.stack([(grid[i, :, j] + grid[j, :, i].T) * 0.5 for i, j in LOWER])
    theirs = lax.dynamic_slice_in_dim(lower, (1 - core) * 5, 5, 0)
    part = lax.dynamic_slice_in_dim(lower, core * 5, 5, 0) + shift(theirs, "core", 1)
    part = (part + shift(part, "zh", 1)).reshape(5 * BLOCK, BLOCK)
    half = 5 * BLOCK // 2
    part = jnp.concatenate(
        [from_root(part[:half], "x", "y", away), from_root(part[half:], "y", "x", away)]
    ).reshape(5, BLOCK, BLOCK)
    other = shift(part, "core", 1)
    parts = jnp.concatenate(
        [jnp.where(core == 0, part, other), jnp.where(core == 0, other, part)]
    )
    rows = []
    for i in range(4):
        rows.append(
            jnp.concatenate(
                [parts[LOWER.index((max(i, j), min(i, j)))] for j in range(4)], axis=1
            )
        )
    diagonal = jnp.concatenate(rows, axis=0)

    product = low_rank(left_u, earlier_right_factors, pivot_right)

    def for_column(z, c):
        block = lax.dynamic_slice_in_dim(pivot_left, (2 * z + c) * BLOCK, BLOCK, 0)
        return times_transposed(product, block)

    far = for_column(1 - zh, core) + shift(for_column(1 - zh, 1 - core), "core", 1)
    near = for_column(zh, core) + shift(for_column(zh, 1 - core), "core", 1)
    updated = panel_tiles - near - shift(far, "zh", 1)
    updated_z = shift(updated, "zh", 1)
    updated_c = shift(updated, "core", 1)
    updated_zc = shift(updated_z, "core", 1)

    factor = lax.linalg.cholesky(diagonal, symmetrize_input=False)
    inverse = lax.linalg.triangular_solve(
        factor, jnp.eye(TILE, dtype=jnp.float32), left_side=True, lower=True
    )
    rows_inv = lax.dynamic_slice_in_dim(inverse, my_col * BLOCK, BLOCK, 0)

    def solved_part(block, z, c):
        return lax.dot_general(
            block,
            lax.dynamic_slice_in_dim(rows_inv, (2 * z + c) * BLOCK, BLOCK, 1),
            (((1,), (1,)), ((), ())),
            precision=lax.Precision.HIGHEST,
            preferred_element_type=jnp.float32,
        )

    solved = solved_part(updated, zh, core) + solved_part(updated_z, 1 - zh, core)
    solved = solved + solved_part(updated_c, zh, 1 - core)
    solved = solved + solved_part(updated_zc, 1 - zh, 1 - core)
    factor_cols = lax.dynamic_slice_in_dim(factor, my_col * BLOCK, BLOCK, 1)
    row_tiles = jnp.arange(TILE_DEV * TILE, dtype=jnp.int32) // TILE
    chosen = jnp.logical_and(lax.axis_index(ROW) == owner, row_tiles == slot)
    return jnp.where(chosen[:, None], jnp.tile(factor_cols, (TILE_DEV, 1)), solved)


def solution(mesh):
    split = Mesh(mesh.devices.reshape(2, 4, 4, 2, 2), ("zl", "y", "x", "zh", "core"))
    return jax.shard_map(
        local,
        mesh=split,
        in_specs=(P(ROW, COL), P(ROW, COL), P(ROW, COL), P()),
        out_specs=P(ROW, COL),
        check_vma=False,
    )
```

```python
import functools

import jax
import jax.numpy as jnp
from jax import lax
from jax.experimental import pallas as pl
from jax.experimental.pallas import tpu as pltpu
from jax.sharding import Mesh
from jax.sharding import PartitionSpec as P

TILE = 1024
RANK = 256
TILE_DEV = 2
COL_DEV = 6
BLOCK = 256
ROW = ("zl", "y", "x")
COL = ("zh", "core")
UPPER = ((0, 0), (1, 1), (2, 2), (0, 1), (0, 2), (3, 3), (1, 2), (2, 3), (1, 3), (0, 3))
NB = 128
STRIP = 32
F32 = jnp.float32
HIGHEST = lax.Precision.HIGHEST


def shift(value, axis, step):
    devices = lax.axis_size(axis)
    return lax.ppermute(value, axis, [(i, (i + step) % devices) for i in range(devices)])


def dot(a, b, ca, cb, precision=None):
    return lax.dot_general(
        a, b, (((ca,), (cb,)), ((), ())), precision=precision, preferred_element_type=F32
    )


def params():
    return pltpu.CompilerParams(vmem_limit_bytes=48 << 20)


def join_kernel(away_ref, *refs):
    out = refs[-1]
    rows = refs[0].shape[0]
    for k in range(4):
        start = pl.multiple_of(((away_ref[0] - k) & 3) * rows, rows)
        out[pl.ds(start, rows), :] = refs[k][...]


def join(got, away):
    rows, columns = got[0].shape
    size = 4 * rows * columns * got[0].dtype.itemsize
    return pl.pallas_call(
        join_kernel,
        out_shape=jax.ShapeDtypeStruct((4 * rows, columns), got[0].dtype),
        in_specs=[pl.BlockSpec(memory_space=pltpu.SMEM)]
        + [pl.BlockSpec(memory_space=pltpu.VMEM)] * 4,
        out_specs=pl.BlockSpec(memory_space=pltpu.VMEM),
        compiler_params=params(),
        cost_estimate=pl.CostEstimate(flops=0, bytes_accessed=2 * size, transcendentals=0),
    )(away.reshape(1), *got)


def scatter(parts, axis, away):
    got = [parts[0]] + [shift(parts[k], axis, k) for k in (1, 2, 3)]
    return lax.select_n(away, *got)


def quarters(value):
    rows = value.shape[0] // 4
    return [value[k * rows : (k + 1) * rows] for k in range(4)]


def pieces(piece, axis):
    return [piece] + [shift(piece, axis, k) for k in (1, 2, 3)]


def from_root(parts, first, second, away):
    piece = scatter(parts, first, away[first])
    piece = scatter(quarters(piece), second, away[second])
    piece = jnp.where(away["zl"] == 0, piece, shift(piece, "zl", 1))
    piece = join(pieces(piece, second), away[second])
    return pieces(piece, first)


def low_rank_kernel(away_ref, left, right, p0, p1, p2, p3, out):
    inner = jnp.zeros((RANK, RANK), F32)
    for k, part in enumerate((p0, p1, p2, p3)):
        start = pl.multiple_of(((away_ref[0] - k) & 3) * BLOCK, BLOCK)
        inner += dot(right[pl.ds(start, BLOCK), :], part[...], 0, 0)
    out[...] = dot(left[...], inner.astype(jnp.bfloat16), 1, 0).astype(jnp.bfloat16)


def low_rank(left, right, parts, away):
    rows, columns = left.shape
    tile = pl.BlockSpec((TILE, RANK), lambda t, j, s: (t, j))
    part = pl.BlockSpec((BLOCK, RANK), lambda t, j, s: (0, j))
    return pl.pallas_call(
        low_rank_kernel,
        out_shape=jax.ShapeDtypeStruct((rows, columns), jnp.bfloat16),
        grid_spec=pltpu.PrefetchScalarGridSpec(
            num_scalar_prefetch=1,
            grid=(rows // TILE, columns // RANK),
            in_specs=[tile, tile, part, part, part, part],
            out_specs=tile,
        ),
        compiler_params=params(),
        cost_estimate=pl.CostEstimate(
            flops=4 * rows * columns * RANK, bytes_accessed=6 * rows * columns, transcendentals=0
        ),
    )(away.reshape(1), left, right, *parts)


def pivot_kernel(where_ref, left, right, panel, out, total):
    j = pl.program_id(0)

    @pl.when(j == 0)
    def _():
        total[...] = jnp.zeros_like(total)
        start = pl.multiple_of(where_ref[1] * BLOCK, BLOCK)
        total[:, pl.ds(start, BLOCK)] = panel[...]

    inner = dot(right[...], right[...], 0, 0).astype(jnp.bfloat16)
    product = dot(left[...], inner, 1, 0).astype(jnp.bfloat16)
    total[...] -= dot(product, left[...], 1, 1)

    @pl.when(j == COL_DEV - 1)
    def _():
        core = where_ref[2]
        for b, (r, c) in enumerate(UPPER):
            above = total[r * BLOCK : (r + 1) * BLOCK, c * BLOCK : (c + 1) * BLOCK]
            below = total[c * BLOCK : (c + 1) * BLOCK, r * BLOCK : (r + 1) * BLOCK]
            out[jnp.where(core == b // 5, 0, 1), b % 5] = (above + below.T) * 0.5


def pivot_update(left, right, panel, slot, my_col, core):
    tile = pl.BlockSpec((TILE, RANK), lambda j, s: (s[0], j))
    return pl.pallas_call(
        pivot_kernel,
        out_shape=jax.ShapeDtypeStruct((2, 5, BLOCK, BLOCK), F32),
        grid_spec=pltpu.PrefetchScalarGridSpec(
            num_scalar_prefetch=1,
            grid=(COL_DEV,),
            in_specs=[tile, tile, pl.BlockSpec((TILE, BLOCK), lambda j, s: (s[0], 0))],
            out_specs=pl.BlockSpec((2, 5, BLOCK, BLOCK), lambda j, s: (0, 0, 0, 0)),
            scratch_shapes=[pltpu.VMEM((TILE, TILE), F32)],
        ),
        compiler_params=params(),
        cost_estimate=pl.CostEstimate(
            flops=5 * 10**9, bytes_accessed=10 * 2**20, transcendentals=0
        ),
    )(jnp.stack([slot, my_col, core]), left, right, panel)


def factor_kernel(where_ref, mine, other, factor_out, inverse_out, u_ref, x_ref, m_ref, f_ref):
    for b, (r, c) in enumerate(UPPER):
        block = jnp.where(where_ref[1] == b // 5, mine[b % 5], other[b % 5])
        u_ref[r * BLOCK : (r + 1) * BLOCK, c * BLOCK : (c + 1) * BLOCK] = block
    x_ref[...] = jnp.zeros_like(x_ref)
    row = lax.broadcasted_iota(jnp.int32, (NB, NB), 0)
    column = lax.broadcasted_iota(jnp.int32, (NB, NB), 1)
    strip_row = lax.broadcasted_iota(jnp.int32, (STRIP, NB), 0)
    for k in range(TILE // NB):
        k0, k1 = k * NB, (k + 1) * NB
        m_ref[:, :NB] = u_ref[k0:k1, k0:k1]
        m_ref[:, NB:] = jnp.where(row == column, 1.0, 0.0).astype(F32)

        def strip(t, carry):
            start = pl.multiple_of(t * STRIP, STRIP)
            ps = m_ref[pl.ds(start, STRIP), :NB]
            pi = m_ref[pl.ds(start, STRIP), NB:]
            turned = pltpu.roll(ps, NB - start, 1)
            c = [jnp.broadcast_to(turned[:, j : j + 1], (STRIP, NB)) for j in range(STRIP)]
            for j in range(STRIP):
                inv = lax.rsqrt(jnp.broadcast_to(c[j][j : j + 1, :], (STRIP, NB)))
                col = c[j] * inv
                for q in range(j + 1, STRIP):
                    c[q] = c[q] - col * jnp.broadcast_to(col[q : q + 1, :], (STRIP, NB))
                us = jnp.broadcast_to(ps[j : j + 1, :], (STRIP, NB)) * inv
                ui = jnp.broadcast_to(pi[j : j + 1, :], (STRIP, NB)) * inv
                below = jnp.where(strip_row > j, col, 0.0)
                ps = jnp.where(strip_row == j, us, ps - below * us)
                pi = jnp.where(strip_row == j, ui, pi - below * ui)
            f_ref[pl.ds(start, STRIP), :NB] = ps
            f_ref[pl.ds(start, STRIP), NB:] = pi
            m_ref[:, :NB] -= dot(ps, ps, 0, 0, HIGHEST)
            m_ref[:, NB:] -= dot(ps, pi, 0, 0, HIGHEST)
            return carry

        lax.fori_loop(0, NB // STRIP, strip, 0)
        xk = f_ref[:, NB:]
        u_ref[k0:k1, k0:k1] = f_ref[:, :NB]
        if k:
            x_ref[k0:k1, :k0] = dot(xk, x_ref[k0:k1, :k0], 1, 0, HIGHEST)
        x_ref[k0:k1, k0:k1] = xk
        if k1 < TILE:
            w = dot(xk, u_ref[k0:k1, k1:], 1, 0, HIGHEST)
            u_ref[k0:k1, k1:] = w
            for i in range(k + 1, TILE // NB):
                wi = w[:, i * NB - k1 : (i + 1) * NB - k1]
                u_ref[i * NB : (i + 1) * NB, i * NB :] -= dot(
                    wi, w[:, i * NB - k1 :], 0, 0, HIGHEST
                )
                x_ref[i * NB : (i + 1) * NB, :k1] -= dot(wi, x_ref[k0:k1, :k1], 0, 0, HIGHEST)
    first = pl.multiple_of(where_ref[0] * BLOCK, BLOCK)
    inverse_out[...] = x_ref[pl.ds(first, BLOCK), :]
    for b in range(4):
        block = u_ref[pl.ds(first, BLOCK), b * BLOCK : (b + 1) * BLOCK].T
        r = lax.broadcasted_iota(jnp.int32, (BLOCK, BLOCK), 0) + b * BLOCK
        c = lax.broadcasted_iota(jnp.int32, (BLOCK, BLOCK), 1) + first
        factor_out[b * BLOCK : (b + 1) * BLOCK, :] = jnp.where(r >= c, block, 0.0)


def factor_and_inverse(mine, other, my_col, core):
    return pl.pallas_call(
        factor_kernel,
        out_shape=(
            jax.ShapeDtypeStruct((TILE, BLOCK), F32),
            jax.ShapeDtypeStruct((BLOCK, TILE), F32),
        ),
        in_specs=[pl.BlockSpec(memory_space=pltpu.SMEM)]
        + [pl.BlockSpec(memory_space=pltpu.VMEM)] * 2,
        out_specs=[pl.BlockSpec(memory_space=pltpu.VMEM)] * 2,
        scratch_shapes=[pltpu.VMEM((TILE, TILE), F32)] * 2 + [pltpu.VMEM((NB, 2 * NB), F32)] * 2,
        compiler_params=params(),
        cost_estimate=pl.CostEstimate(
            flops=50 * 10**9, bytes_accessed=5 * 2**20, transcendentals=0
        ),
    )(jnp.stack([my_col, core]), mine, other)


def local(panel_tiles, left_u, earlier_right_factors, tile_global_index):
    tile_count = tile_global_index.shape[0]
    pivot_position = jnp.sum(
        jnp.where(tile_global_index == 0, jnp.arange(tile_count, dtype=jnp.int32), 0)
    )
    owner = pivot_position // TILE_DEV
    slot = pivot_position % TILE_DEV
    away = {
        "x": (lax.axis_index("x") - owner % 4) % 4,
        "y": (lax.axis_index("y") - owner // 4 % 4) % 4,
        "zl": (lax.axis_index("zl") - owner // 16) % 2,
    }
    zh, core = lax.axis_index("zh"), lax.axis_index("core")
    my_col = lax.axis_index(COL)

    def slot_quarters(value):
        return [
            lax.dynamic_slice_in_dim(value, slot * TILE + k * BLOCK, BLOCK, 0) for k in range(4)
        ]

    right_parts = from_root(slot_quarters(earlier_right_factors), "x", "y", away)
    left_parts = from_root(slot_quarters(left_u), "y", "x", away)

    upper = pivot_update(left_u, earlier_right_factors, panel_tiles, slot, my_col, core)
    part = upper[0] + shift(upper[1], "core", 1)
    part = (part + shift(part, "zh", 1)).reshape(5 * BLOCK, BLOCK)
    half = 5 * BLOCK // 2
    one = join(from_root(quarters(part[:half]), "x", "y", away), away["x"])
    two = join(from_root(quarters(part[half:]), "y", "x", away), away["y"])
    mine = jnp.concatenate([one, two]).reshape(5, BLOCK, BLOCK)
    other = shift(mine, "core", 1)

    product = low_rank(left_u, earlier_right_factors, right_parts, away["x"])
    pivot_left = jnp.stack(left_parts)

    def for_column(z, c):
        block = lax.dynamic_index_in_dim(pivot_left, (away["y"] - 2 * z - c) % 4, 0, False)
        return dot(product, block, 1, 1)

    far = for_column(1 - zh, core) + shift(for_column(1 - zh, 1 - core), "core", 1)
    near = for_column(zh, core) + shift(for_column(zh, 1 - core), "core", 1)
    updated = panel_tiles - near - shift(far, "zh", 1)
    updated_z = shift(updated, "zh", 1)
    updated_c = shift(updated, "core", 1)
    updated_zc = shift(updated_z, "core", 1)

    factor_cols, rows_inv = factor_and_inverse(mine, other, my_col, core)

    def solved_part(block, z, c):
        inv = lax.dynamic_slice_in_dim(rows_inv, (2 * z + c) * BLOCK, BLOCK, 1)
        return dot(block, inv, 1, 1, lax.Precision.HIGH)

    solved = solved_part(updated, zh, core) + solved_part(updated_c, zh, 1 - core)
    solved = solved + solved_part(updated_z, 1 - zh, core)
    solved = solved + solved_part(updated_zc, 1 - zh, 1 - core)
    row_tiles = jnp.arange(TILE_DEV * TILE, dtype=jnp.int32) // TILE
    chosen = jnp.logical_and(lax.axis_index(ROW) == owner, row_tiles == slot)
    return jnp.where(chosen[:, None], jnp.tile(factor_cols, (TILE_DEV, 1)), solved)


def solution(mesh):
    split = Mesh(mesh.devices.reshape(2, 4, 4, 2, 2), ("zl", "y", "x", "zh", "core"))
    return jax.shard_map(
        local,
        mesh=split,
        in_specs=(P(ROW, COL), P(ROW, COL), P(ROW, COL), P()),
        out_specs=P(ROW, COL),
        check_vma=False,
    )
```

```python
import functools

import jax
import jax.numpy as jnp
from jax import lax
from jax.experimental import pallas as pl
from jax.experimental.pallas import tpu as pltpu
from jax.sharding import Mesh
from jax.sharding import PartitionSpec as P

TILE = 1024
RANK = 256
TILE_DEV = 2
COL_DEV = 6
BLOCK = 256
HALF = 512
ROW = ("zl", "y", "x")
COL = ("zh", "core")
UPPER = ((0, 0), (1, 1), (2, 2), (0, 1), (0, 2), (3, 3), (1, 2), (2, 3), (1, 3), (0, 3))
NB = 128
STRIP = 32
F32 = jnp.float32
HIGHEST = lax.Precision.HIGHEST


def shift(value, axis, step):
    devices = lax.axis_size(axis)
    return lax.ppermute(value, axis, [(i, (i + step) % devices) for i in range(devices)])


def dot(a, b, ca, cb, precision=None):
    return lax.dot_general(
        a, b, (((ca,), (cb,)), ((), ())), precision=precision, preferred_element_type=F32
    )


def params():
    return pltpu.CompilerParams(vmem_limit_bytes=48 << 20)


def place_kernel(axis, where_ref, *refs):
    out = refs[-1]
    for k, ref in enumerate(refs[:-1]):
        size = ref.shape[axis]
        part = pl.ds(pl.multiple_of(where_ref[k] * size, size), size)
        if axis == 0:
            out[part, :] = ref[...]
        else:
            out[:, part] = ref[...]


def place(values, where, axis=0):
    shape = list(values[0].shape)
    shape[axis] *= len(values)
    size = shape[0] * shape[1] * values[0].dtype.itemsize
    return pl.pallas_call(
        functools.partial(place_kernel, axis),
        out_shape=jax.ShapeDtypeStruct(shape, values[0].dtype),
        in_specs=[pl.BlockSpec(memory_space=pltpu.SMEM)]
        + [pl.BlockSpec(memory_space=pltpu.VMEM)] * len(values),
        out_specs=pl.BlockSpec(memory_space=pltpu.VMEM),
        compiler_params=params(),
        cost_estimate=pl.CostEstimate(flops=0, bytes_accessed=2 * size, transcendentals=0),
    )(where, *values)


def in_step(*values):
    return lax.optimization_barrier(values)


def quarters(value):
    rows = value.shape[0] // 4
    return [value[k * rows : (k + 1) * rows] for k in range(4)]


def sends(parts, axis):
    return [parts[0]] + [shift(parts[k], axis, k) for k in (1, 2, 3)]


def pieces(piece, axis):
    return [piece] + [shift(piece, axis, k) for k in (1, 2, 3)]


def low_rank_kernel(where_ref, left, right, p0, p1, p2, p3, out, pivot):
    for k, part in enumerate((p0, p1, p2, p3)):
        start = pl.multiple_of(where_ref[k] * BLOCK, BLOCK)
        pivot[:, pl.ds(start, BLOCK)] = part[...].T
    for t in range(TILE_DEV):
        rows = slice(t * TILE, (t + 1) * TILE)
        inner = dot(pivot[...], right[rows, :], 1, 0).astype(jnp.bfloat16)
        out[rows, :] = dot(left[rows, :], inner, 1, 1).astype(jnp.bfloat16)


def low_rank(left, right, parts, where):
    rows, columns = left.shape
    both = pl.BlockSpec((rows, RANK), lambda j, s: (0, j))
    part = pl.BlockSpec((BLOCK, RANK), lambda j, s: (0, j))
    return pl.pallas_call(
        low_rank_kernel,
        out_shape=jax.ShapeDtypeStruct((rows, columns), jnp.bfloat16),
        grid_spec=pltpu.PrefetchScalarGridSpec(
            num_scalar_prefetch=1,
            grid=(columns // RANK,),
            in_specs=[both, both, part, part, part, part],
            out_specs=both,
            scratch_shapes=[pltpu.VMEM((RANK, TILE), jnp.bfloat16)],
        ),
        compiler_params=params(),
        cost_estimate=pl.CostEstimate(
            flops=4 * rows * columns * RANK, bytes_accessed=6 * rows * columns, transcendentals=0
        ),
    )(where, left, right, *parts)


def pivot_kernel(where_ref, left, right, panel, out, total):
    j = pl.program_id(0)

    @pl.when(j == 0)
    def _():
        total[...] = jnp.zeros_like(total)
        start = pl.multiple_of(where_ref[1] * BLOCK, BLOCK)
        total[:, pl.ds(start, BLOCK)] = panel[...]

    inner = dot(right[...], right[...], 0, 0).astype(jnp.bfloat16)
    product = dot(left[...], inner, 1, 0).astype(jnp.bfloat16)
    total[...] -= dot(product, left[...], 1, 1)

    @pl.when(j == COL_DEV - 1)
    def _():
        core = where_ref[2]
        for b, (r, c) in enumerate(UPPER):
            above = total[r * BLOCK : (r + 1) * BLOCK, c * BLOCK : (c + 1) * BLOCK]
            below = total[c * BLOCK : (c + 1) * BLOCK, r * BLOCK : (r + 1) * BLOCK]
            out[jnp.where(core == b // 5, 0, 1), b % 5] = (above + below.T) * 0.5


def pivot_update(left, right, panel, slot, my_col, core):
    tile = pl.BlockSpec((TILE, RANK), lambda j, s: (s[0], j))
    return pl.pallas_call(
        pivot_kernel,
        out_shape=jax.ShapeDtypeStruct((2, 5, BLOCK, BLOCK), F32),
        grid_spec=pltpu.PrefetchScalarGridSpec(
            num_scalar_prefetch=1,
            grid=(COL_DEV,),
            in_specs=[tile, tile, pl.BlockSpec((TILE, BLOCK), lambda j, s: (s[0], 0))],
            out_specs=pl.BlockSpec((2, 5, BLOCK, BLOCK), lambda j, s: (0, 0, 0, 0)),
            scratch_shapes=[pltpu.VMEM((TILE, TILE), F32)],
        ),
        compiler_params=params(),
        cost_estimate=pl.CostEstimate(
            flops=5 * 10**9, bytes_accessed=10 * 2**20, transcendentals=0
        ),
    )(jnp.stack([slot, my_col, core]), left, right, panel)


def factor_kernel(where_ref, mine, other, factor_out, inverse_out, u_ref, x_ref, m_ref, f_ref):
    for b, (r, c) in enumerate(UPPER):
        block = jnp.where(where_ref[0] == b // 5, mine[b % 5], other[b % 5])
        u_ref[r * BLOCK : (r + 1) * BLOCK, c * BLOCK : (c + 1) * BLOCK] = block
    x_ref[...] = jnp.zeros_like(x_ref)
    row = lax.broadcasted_iota(jnp.int32, (NB, NB), 0)
    column = lax.broadcasted_iota(jnp.int32, (NB, NB), 1)
    strip_row = lax.broadcasted_iota(jnp.int32, (STRIP, NB), 0)
    for k in range(TILE // NB):
        k0, k1 = k * NB, (k + 1) * NB
        m_ref[:, :NB] = u_ref[k0:k1, k0:k1]
        m_ref[:, NB:] = jnp.where(row == column, 1.0, 0.0).astype(F32)

        def strip(t, carry):
            start = pl.multiple_of(t * STRIP, STRIP)
            ps = m_ref[pl.ds(start, STRIP), :NB]
            pi = m_ref[pl.ds(start, STRIP), NB:]
            turned = pltpu.roll(ps, NB - start, 1)
            c = [jnp.broadcast_to(turned[:, j : j + 1], (STRIP, NB)) for j in range(STRIP)]
            for j in range(STRIP):
                inv = lax.rsqrt(jnp.broadcast_to(c[j][j : j + 1, :], (STRIP, NB)))
                col = c[j] * inv
                for q in range(j + 1, STRIP):
                    c[q] = c[q] - col * jnp.broadcast_to(col[q : q + 1, :], (STRIP, NB))
                us = jnp.broadcast_to(ps[j : j + 1, :], (STRIP, NB)) * inv
                ui = jnp.broadcast_to(pi[j : j + 1, :], (STRIP, NB)) * inv
                below = jnp.where(strip_row > j, col, 0.0)
                ps = jnp.where(strip_row == j, us, ps - below * us)
                pi = jnp.where(strip_row == j, ui, pi - below * ui)
            f_ref[pl.ds(start, STRIP), :NB] = ps
            f_ref[pl.ds(start, STRIP), NB:] = pi
            m_ref[:, :NB] -= dot(ps, ps, 0, 0, HIGHEST)
            m_ref[:, NB:] -= dot(ps, pi, 0, 0, HIGHEST)
            return carry

        lax.fori_loop(0, NB // STRIP, strip, 0)
        xk = f_ref[:, NB:]
        u_ref[k0:k1, k0:k1] = f_ref[:, :NB]
        if k:
            x_ref[k0:k1, :k0] = dot(xk, x_ref[k0:k1, :k0], 1, 0, HIGHEST)
        x_ref[k0:k1, k0:k1] = xk
        if k1 < TILE:
            w = dot(xk, u_ref[k0:k1, k1:], 1, 0, HIGHEST)
            u_ref[k0:k1, k1:] = w
            for i in range(k + 1, TILE // NB):
                wi = w[:, i * NB - k1 : (i + 1) * NB - k1]
                u_ref[i * NB : (i + 1) * NB, i * NB :] -= dot(
                    wi, w[:, i * NB - k1 :], 0, 0, HIGHEST
                )
                x_ref[i * NB : (i + 1) * NB, :k1] -= dot(wi, x_ref[k0:k1, :k1], 0, 0, HIGHEST)
    inverse_out[...] = x_ref[...]
    first = pl.multiple_of(where_ref[0] * HALF, HALF)
    for b in range(4):
        block = u_ref[b * BLOCK : (b + 1) * BLOCK, pl.ds(first, HALF)].T
        r = lax.broadcasted_iota(jnp.int32, (HALF, BLOCK), 0) + first
        c = lax.broadcasted_iota(jnp.int32, (HALF, BLOCK), 1) + b * BLOCK
        factor_out[:, b * BLOCK : (b + 1) * BLOCK] = jnp.where(r >= c, block, 0.0)


def factor_and_inverse(mine, other, core):
    return pl.pallas_call(
        factor_kernel,
        out_shape=(
            jax.ShapeDtypeStruct((HALF, TILE), F32),
            jax.ShapeDtypeStruct((TILE, TILE), F32),
        ),
        in_specs=[pl.BlockSpec(memory_space=pltpu.SMEM)]
        + [pl.BlockSpec(memory_space=pltpu.VMEM)] * 2,
        out_specs=[pl.BlockSpec(memory_space=pltpu.VMEM)] * 2,
        scratch_shapes=[pltpu.VMEM((TILE, TILE), F32)] * 2 + [pltpu.VMEM((NB, 2 * NB), F32)] * 2,
        compiler_params=params(),
        cost_estimate=pl.CostEstimate(
            flops=50 * 10**9, bytes_accessed=5 * 2**20, transcendentals=0
        ),
    )(core.reshape(1), mine, other)


def local(panel_tiles, left_u, earlier_right_factors, tile_global_index):
    tile_count = tile_global_index.shape[0]
    pivot_position = jnp.sum(
        jnp.where(tile_global_index == 0, jnp.arange(tile_count, dtype=jnp.int32), 0)
    )
    owner = pivot_position >> 1
    slot = pivot_position & 1
    away = {
        "x": (lax.axis_index("x") - owner) & 3,
        "y": (lax.axis_index("y") - (owner >> 2)) & 3,
        "zl": (lax.axis_index("zl") - (owner >> 4)) & 1,
    }
    zh, core = lax.axis_index("zh"), lax.axis_index("core")
    my_col = lax.axis_index(COL)

    def slot_quarters(value):
        return [
            lax.dynamic_slice_in_dim(value, slot * TILE + k * BLOCK, BLOCK, 0) for k in range(4)
        ]

    where = {a: jnp.stack([(away[a] - k) & 3 for k in range(4)]) for a in ("x", "y")}
    both = jnp.concatenate([where["x"], where["y"] + 4])
    quad = jnp.stack([2 * zh + core, 2 * zh + 1 - core, 2 - 2 * zh + core, 3 - 2 * zh - core])
    holds = away["zl"] == 0

    def slot_quarters(value):
        return [
            lax.dynamic_slice_in_dim(value, slot * TILE + k * BLOCK, BLOCK, 0) for k in range(4)
        ]

    def rows_of(value, z, c):
        return lax.dynamic_slice_in_dim(value, (2 * z + c) * HALF, HALF, 0)

    v = sends(slot_quarters(earlier_right_factors), "x")
    u = sends(slot_quarters(left_u), "y")

    upper = pivot_update(left_u, earlier_right_factors, panel_tiles, slot, my_col, core)
    s = upper[0] + shift(upper[1], "core", 1)
    v, u, _ = in_step(v, u, s)
    s = (s + shift(s, "zh", 1)).reshape(5 * BLOCK, BLOCK)
    half = 5 * BLOCK // 2

    v, u = in_step(lax.select_n(away["x"], *v), lax.select_n(away["y"], *u))
    v, u = sends(quarters(v), "y"), sends(quarters(u), "x")
    v, u, s = in_step(lax.select_n(away["y"], *v), lax.select_n(away["x"], *u), s)
    s, t = sends(quarters(s[:half]), "x"), sends(quarters(s[half:]), "y")
    v = jnp.where(holds, v, shift(v, "zl", 1))
    u = jnp.where(holds, u, shift(u, "zl", 1))
    s, t = lax.select_n(away["x"], *s), lax.select_n(away["y"], *t)
    v, u, s, t = in_step(v, u, s, t)
    s, t = sends(quarters(s), "y"), sends(quarters(t), "x")
    v, u = pieces(v, "y"), pieces(u, "x")
    s, t = lax.select_n(away["y"], *s), lax.select_n(away["x"], *t)
    v, u = place(v, where["y"]), place(u, where["x"])
    v, u, s, t = in_step(v, u, s, t)
    s, t = jnp.where(holds, s, shift(s, "zl", 1)), jnp.where(holds, t, shift(t, "zl", 1))
    v, u = pieces(v, "x"), pieces(u, "y")
    s, t = place(pieces(s, "y"), where["y"]), place(pieces(t, "x"), where["x"])
    mine = place(pieces(s, "x") + pieces(t, "y"), both).reshape(5, BLOCK, BLOCK)
    other = shift(mine, "core", 1)

    tiles = [lax.dynamic_slice_in_dim(panel_tiles, z * TILE, TILE, 0) for z in (zh, 1 - zh)]
    tiles = [tiles[0], shift(tiles[1], "zh", 1)]
    own = [lax.dynamic_slice_in_dim(t, core * HALF, HALF, 0) for t in tiles]
    sent = [lax.dynamic_slice_in_dim(t, (1 - core) * HALF, HALF, 0) for t in tiles]
    sent = [shift(t, "core", 1) for t in sent]
    panel_rows = place([own[0], sent[0], own[1], sent[1]], quad, 1)

    product = low_rank(left_u, earlier_right_factors, v, where["x"])
    pivot_left = place(u, where["y"])

    def for_rows(z, c):
        return dot(rows_of(product, z, c), pivot_left, 1, 1)

    far = for_rows(1 - zh, core) + shift(for_rows(1 - zh, 1 - core), "core", 1)
    near = for_rows(zh, core) + shift(for_rows(zh, 1 - core), "core", 1)
    far, mine, other = in_step(far, mine, other)
    far = shift(far, "zh", 1)
    factor_rows, inverse = factor_and_inverse(mine, other, core)
    updated = panel_rows - near - far

    chosen = jnp.logical_and(lax.axis_index(ROW) == owner, slot == zh)

    def solved(z):
        inv = lax.dynamic_slice_in_dim(inverse, z * HALF, HALF, 0)
        fac = lax.dynamic_slice_in_dim(factor_rows, z * HALF, HALF, 1)
        return jnp.where(chosen, fac, dot(updated, inv, 1, 1, lax.Precision.HIGH))

    def column(value, c):
        return lax.dynamic_slice_in_dim(value, c * BLOCK, BLOCK, 1)

    out_far = shift(solved(1 - zh), "zh", 1)
    out_near = solved(zh)
    out = [column(out_near, core), shift(column(out_near, 1 - core), "core", 1)]
    out += [column(out_far, core), shift(column(out_far, 1 - core), "core", 1)]
    return place(out, quad)


def solution(mesh):
    split = Mesh(mesh.devices.reshape(2, 4, 4, 2, 2), ("zl", "y", "x", "zh", "core"))
    return jax.shard_map(
        local,
        mesh=split,
        in_specs=(P(ROW, COL), P(ROW, COL), P(ROW, COL), P()),
        out_specs=P(ROW, COL),
        check_vma=False,
    )
```

```python
import functools

import jax
import jax.numpy as jnp
from jax import lax
from jax.experimental import pallas as pl
from jax.experimental.pallas import tpu as pltpu
from jax.sharding import Mesh
from jax.sharding import PartitionSpec as P

TILE = 1024
RANK = 256
TILE_DEV = 2
COL_DEV = 6
BLOCK = 256
HALF = 512
ROW = ("zl", "y", "x")
COL = ("zh", "core")
UPPER = ((0, 0), (1, 1), (2, 2), (0, 1), (0, 2), (3, 3), (1, 2), (2, 3), (1, 3), (0, 3))
NB = 128
STRIP = 32
F32 = jnp.float32
HIGHEST = lax.Precision.HIGHEST


def shift(value, axis, step):
    devices = lax.axis_size(axis)
    return lax.ppermute(value, axis, [(i, (i + step) % devices) for i in range(devices)])


def dot(a, b, ca, cb, precision=None):
    return lax.dot_general(
        a, b, (((ca,), (cb,)), ((), ())), precision=precision, preferred_element_type=F32
    )


def params():
    return pltpu.CompilerParams(vmem_limit_bytes=48 << 20)


def place_kernel(axis, where_ref, *refs):
    out = refs[-1]
    for k, ref in enumerate(refs[:-1]):
        size = ref.shape[axis]
        part = pl.ds(pl.multiple_of(where_ref[k] * size, size), size)
        if axis == 0:
            out[part, :] = ref[...]
        else:
            out[:, part] = ref[...]


def place(values, where, axis=0):
    shape = list(values[0].shape)
    shape[axis] *= len(values)
    size = shape[0] * shape[1] * values[0].dtype.itemsize
    return pl.pallas_call(
        functools.partial(place_kernel, axis),
        out_shape=jax.ShapeDtypeStruct(shape, values[0].dtype),
        in_specs=[pl.BlockSpec(memory_space=pltpu.SMEM)]
        + [pl.BlockSpec(memory_space=pltpu.VMEM)] * len(values),
        out_specs=pl.BlockSpec(memory_space=pltpu.VMEM),
        compiler_params=params(),
        cost_estimate=pl.CostEstimate(flops=0, bytes_accessed=2 * size, transcendentals=0),
    )(where, *values)


def in_step(*values):
    return lax.optimization_barrier(values)


def quarters(value):
    rows = value.shape[0] // 4
    return [value[k * rows : (k + 1) * rows] for k in range(4)]


def sends(parts, axis):
    return [parts[0]] + [shift(parts[k], axis, k) for k in (1, 2, 3)]


def sends_two(v, u, v_axis, u_axis, after):
    v1, v3 = shift(v[1], v_axis, 1), shift(v[3], v_axis, 3)
    u1, u3 = shift(u[1], u_axis, 1), shift(u[3], u_axis, 3)
    v2, u2, v1, v3, u1, u3, after = in_step(v[2], u[2], v1, v3, u1, u3, after)
    v2, u2 = shift(v2, v_axis, 2), shift(u2, u_axis, 2)
    return [v[0], v1, v2, v3], [u[0], u1, u2, u3], after


def pieces(piece, axis):
    return sends([piece] * 4, axis)


def low_rank_kernel(where_ref, left, right, right_pieces, left_pieces, out, pivot_left, pivot):
    size = left_pieces.shape[1]
    for k in range(left_pieces.shape[0]):
        x, y = where_ref[k], where_ref[16 + k]
        pivot[pl.ds(pl.multiple_of((4 * x + y) * size, size), size), :] = right_pieces[k]
        pivot_left[pl.ds(pl.multiple_of((4 * y + x) * size, size), size), :] = left_pieces[k]
    turned = pivot[...].T
    for t in range(TILE_DEV):
        rows = slice(t * TILE, (t + 1) * TILE)
        inner = dot(turned, right[rows, :], 1, 0).astype(jnp.bfloat16)
        out[rows, :] = dot(left[rows, :], inner, 1, 1).astype(jnp.bfloat16)


def low_rank(left, right, gathered, where):
    rows, columns = left.shape
    count, size = gathered.shape[:2]
    steps = columns // RANK
    both = pl.BlockSpec((rows, RANK), lambda j, s: (0, j))
    return pl.pallas_call(
        low_rank_kernel,
        out_shape=(
            jax.ShapeDtypeStruct((rows, columns), jnp.bfloat16),
            jax.ShapeDtypeStruct((TILE, columns), jnp.bfloat16),
        ),
        grid_spec=pltpu.PrefetchScalarGridSpec(
            num_scalar_prefetch=1,
            grid=(steps,),
            in_specs=[
                both,
                both,
                pl.BlockSpec((count, size, RANK), lambda j, s: (0, 0, j)),
                pl.BlockSpec((count, size, RANK), lambda j, s: (0, 0, j + steps)),
            ],
            out_specs=[both, pl.BlockSpec((TILE, RANK), lambda j, s: (0, j))],
            scratch_shapes=[pltpu.VMEM((TILE, RANK), jnp.bfloat16)],
        ),
        compiler_params=params(),
        cost_estimate=pl.CostEstimate(
            flops=4 * rows * columns * RANK, bytes_accessed=8 * rows * columns, transcendentals=0
        ),
    )(where, left, right, gathered, gathered)


def pivot_kernel(where_ref, left, right, panel, out, total):
    j = pl.program_id(0)

    @pl.when(j == 0)
    def _():
        total[...] = jnp.zeros_like(total)
        start = pl.multiple_of(where_ref[1] * BLOCK, BLOCK)
        total[:, pl.ds(start, BLOCK)] = panel[...]

    inner = dot(right[...], right[...], 0, 0).astype(jnp.bfloat16)
    product = dot(left[...], inner, 1, 0).astype(jnp.bfloat16)
    total[...] -= dot(product, left[...], 1, 1)

    @pl.when(j == COL_DEV - 1)
    def _():
        core = where_ref[2]
        for b, (r, c) in enumerate(UPPER):
            above = total[r * BLOCK : (r + 1) * BLOCK, c * BLOCK : (c + 1) * BLOCK]
            below = total[c * BLOCK : (c + 1) * BLOCK, r * BLOCK : (r + 1) * BLOCK]
            out[jnp.where(core == b // 5, 0, 1), b % 5] = (above + below.T) * 0.5


def pivot_update(left, right, panel, slot, my_col, core):
    tile = pl.BlockSpec((TILE, RANK), lambda j, s: (s[0], j))
    return pl.pallas_call(
        pivot_kernel,
        out_shape=jax.ShapeDtypeStruct((2, 5, BLOCK, BLOCK), F32),
        grid_spec=pltpu.PrefetchScalarGridSpec(
            num_scalar_prefetch=1,
            grid=(COL_DEV,),
            in_specs=[tile, tile, pl.BlockSpec((TILE, BLOCK), lambda j, s: (s[0], 0))],
            out_specs=pl.BlockSpec((2, 5, BLOCK, BLOCK), lambda j, s: (0, 0, 0, 0)),
            scratch_shapes=[pltpu.VMEM((TILE, TILE), F32)],
        ),
        compiler_params=params(),
        cost_estimate=pl.CostEstimate(
            flops=10**6, bytes_accessed=10**4, transcendentals=0
        ),
    )(jnp.stack([slot, my_col, core]), left, right, panel)


def factor_kernel(where_ref, mine, other, factor_out, inverse_out, u_ref, x_ref, m_ref, f_ref):
    for b, (r, c) in enumerate(UPPER):
        block = jnp.where(where_ref[0] == b // 5, mine[b % 5], other[b % 5])
        u_ref[r * BLOCK : (r + 1) * BLOCK, c * BLOCK : (c + 1) * BLOCK] = block
    x_ref[...] = jnp.zeros_like(x_ref)
    row = lax.broadcasted_iota(jnp.int32, (NB, NB), 0)
    column = lax.broadcasted_iota(jnp.int32, (NB, NB), 1)
    strip_row = lax.broadcasted_iota(jnp.int32, (STRIP, NB), 0)
    for k in range(TILE // NB):
        k0, k1 = k * NB, (k + 1) * NB
        m_ref[:, :NB] = u_ref[k0:k1, k0:k1]
        m_ref[:, NB:] = jnp.where(row == column, 1.0, 0.0).astype(F32)

        def strip(t, carry):
            start = pl.multiple_of(t * STRIP, STRIP)
            ps = m_ref[pl.ds(start, STRIP), :NB]
            pi = m_ref[pl.ds(start, STRIP), NB:]
            turned = pltpu.roll(ps, NB - start, 1)
            c = [jnp.broadcast_to(turned[:, j : j + 1], (STRIP, NB)) for j in range(STRIP)]
            for j in range(STRIP):
                inv = lax.rsqrt(jnp.broadcast_to(c[j][j : j + 1, :], (STRIP, NB)))
                col = c[j] * inv
                for q in range(j + 1, STRIP):
                    c[q] = c[q] - col * jnp.broadcast_to(col[q : q + 1, :], (STRIP, NB))
                us = jnp.broadcast_to(ps[j : j + 1, :], (STRIP, NB)) * inv
                ui = jnp.broadcast_to(pi[j : j + 1, :], (STRIP, NB)) * inv
                below = jnp.where(strip_row > j, col, 0.0)
                ps = jnp.where(strip_row == j, us, ps - below * us)
                pi = jnp.where(strip_row == j, ui, pi - below * ui)
            f_ref[pl.ds(start, STRIP), :NB] = ps
            f_ref[pl.ds(start, STRIP), NB:] = pi
            m_ref[:, :NB] -= dot(ps, ps, 0, 0, HIGHEST)
            m_ref[:, NB:] -= dot(ps, pi, 0, 0, HIGHEST)
            return carry

        lax.fori_loop(0, NB // STRIP, strip, 0)
        xk = f_ref[:, NB:]
        u_ref[k0:k1, k0:k1] = f_ref[:, :NB]
        if k:
            x_ref[k0:k1, :k0] = dot(xk, x_ref[k0:k1, :k0], 1, 0, HIGHEST)
        x_ref[k0:k1, k0:k1] = xk
        if k1 < TILE:
            w = dot(xk, u_ref[k0:k1, k1:], 1, 0, HIGHEST)
            u_ref[k0:k1, k1:] = w
            for i in range(k + 1, TILE // NB):
                wi = w[:, i * NB - k1 : (i + 1) * NB - k1]
                u_ref[i * NB : (i + 1) * NB, i * NB :] -= dot(
                    wi, w[:, i * NB - k1 :], 0, 0, HIGHEST
                )
                x_ref[i * NB : (i + 1) * NB, :k1] -= dot(wi, x_ref[k0:k1, :k1], 0, 0, HIGHEST)
    inverse_out[...] = x_ref[...]
    first = pl.multiple_of(where_ref[0] * HALF, HALF)
    for b in range(4):
        block = u_ref[b * BLOCK : (b + 1) * BLOCK, pl.ds(first, HALF)].T
        r = lax.broadcasted_iota(jnp.int32, (HALF, BLOCK), 0) + first
        c = lax.broadcasted_iota(jnp.int32, (HALF, BLOCK), 1) + b * BLOCK
        factor_out[:, b * BLOCK : (b + 1) * BLOCK] = jnp.where(r >= c, block, 0.0)


def factor_and_inverse(mine, other, core):
    return pl.pallas_call(
        factor_kernel,
        out_shape=(
            jax.ShapeDtypeStruct((HALF, TILE), F32),
            jax.ShapeDtypeStruct((TILE, TILE), F32),
        ),
        in_specs=[pl.BlockSpec(memory_space=pltpu.SMEM)]
        + [pl.BlockSpec(memory_space=pltpu.VMEM)] * 2,
        out_specs=[pl.BlockSpec(memory_space=pltpu.VMEM)] * 2,
        scratch_shapes=[pltpu.VMEM((TILE, TILE), F32)] * 2 + [pltpu.VMEM((NB, 2 * NB), F32)] * 2,
        compiler_params=params(),
        cost_estimate=pl.CostEstimate(
            flops=10**9, bytes_accessed=5 * 2**20, transcendentals=0
        ),
    )(core.reshape(1), mine, other)


def local(panel_tiles, left_u, earlier_right_factors, tile_global_index):
    tile_count = tile_global_index.shape[0]
    pivot_position = jnp.sum(
        jnp.where(tile_global_index == 0, jnp.arange(tile_count, dtype=jnp.int32), 0)
    )
    owner = pivot_position >> 1
    slot = pivot_position & 1
    away = {
        "x": (lax.axis_index("x") - owner) & 3,
        "y": (lax.axis_index("y") - (owner >> 2)) & 3,
        "zl": (lax.axis_index("zl") - (owner >> 4)) & 1,
    }
    zh, core = lax.axis_index("zh"), lax.axis_index("core")
    my_col = lax.axis_index(COL)

    def slot_quarters(value):
        return [
            lax.dynamic_slice_in_dim(value, slot * TILE + k * BLOCK, BLOCK, 0) for k in range(4)
        ]

    where = {a: jnp.stack([(away[a] - k) & 3 for k in range(4)]) for a in ("x", "y")}
    square = jnp.arange(16, dtype=jnp.int32)
    sixteen = jnp.concatenate([(square - owner) & 3, ((square >> 2) - (owner >> 2)) & 3])
    quad = jnp.stack([2 * zh + core, 2 * zh + 1 - core, 2 - 2 * zh + core, 3 - 2 * zh - core])
    holds = away["zl"] == 0

    def slot_quarters(value):
        return [
            lax.dynamic_slice_in_dim(value, slot * TILE + k * BLOCK, BLOCK, 0) for k in range(4)
        ]

    def rows_of(value, z, c):
        return lax.dynamic_slice_in_dim(value, (2 * z + c) * HALF, HALF, 0)

    v, u = slot_quarters(earlier_right_factors), slot_quarters(left_u)
    v, u, slot_after = sends_two(v, u, "x", "y", slot)
    upper = pivot_update(left_u, earlier_right_factors, panel_tiles, slot, my_col, core)
    s = upper[0] + shift(upper[1], "core", 1)
    v, u, _ = in_step(v, u, s)
    s = s + shift(s, "zh", 1)
    v, u = in_step(lax.select_n(away["x"], *v), lax.select_n(away["y"], *u))
    v, u = sends(quarters(v), "y"), sends(quarters(u), "x")
    v, u, s = in_step(lax.select_n(away["y"], *v), lax.select_n(away["x"], *u), s)
    v = jnp.where(holds, v, shift(v, "zl", 1))
    u = jnp.where(holds, u, shift(u, "zl", 1))
    gathered = lax.all_gather(jnp.concatenate([v, u], axis=1), ("y", "x"))

    s = s.reshape(5 * BLOCK, BLOCK)
    s = lax.select_n(away["x"], *sends(quarters(s), "x"))
    s = lax.select_n(away["y"], *sends(quarters(s), "y"))
    s = jnp.where(holds, s, shift(s, "zl", 1))
    s = place(pieces(s, "y"), where["y"])
    mine = place(pieces(s, "x"), where["x"]).reshape(5, BLOCK, BLOCK)
    other = shift(mine, "core", 1)

    tiles = [lax.dynamic_slice_in_dim(panel_tiles, z * TILE, TILE, 0) for z in (zh, 1 - zh)]
    tiles = [tiles[0], shift(tiles[1], "zh", 1)]
    own = [lax.dynamic_slice_in_dim(t, core * HALF, HALF, 0) for t in tiles]
    sent = [lax.dynamic_slice_in_dim(t, (1 - core) * HALF, HALF, 0) for t in tiles]
    sent = [shift(t, "core", 1) for t in sent]
    panel_rows = place([own[0], sent[0], own[1], sent[1]], quad, 1)

    gathered, mine, other, panel_rows = in_step(gathered, mine, other, panel_rows)
    product, pivot_left = low_rank(left_u, earlier_right_factors, gathered, sixteen)

    def for_rows(z, c):
        return dot(rows_of(product, z, c), pivot_left, 1, 1)

    far = for_rows(1 - zh, core) + shift(for_rows(1 - zh, 1 - core), "core", 1)
    near = for_rows(zh, core) + shift(for_rows(zh, 1 - core), "core", 1)
    far, mine, other = in_step(far, mine, other)
    far = shift(far, "zh", 1)
    factor_rows, inverse = factor_and_inverse(mine, other, core)
    updated = panel_rows - near - far

    chosen = jnp.logical_and(lax.axis_index(ROW) == owner, slot == zh)

    def solved(z):
        inv = lax.dynamic_slice_in_dim(inverse, z * HALF, HALF, 0)
        fac = lax.dynamic_slice_in_dim(factor_rows, z * HALF, HALF, 1)
        return jnp.where(chosen, fac, dot(updated, inv, 1, 1, lax.Precision.HIGH))

    def column(value, c):
        return lax.dynamic_slice_in_dim(value, c * BLOCK, BLOCK, 1)

    out_far = shift(solved(1 - zh), "zh", 1)
    out_near = solved(zh)
    out = [column(out_near, core), shift(column(out_near, 1 - core), "core", 1)]
    out += [column(out_far, core), shift(column(out_far, 1 - core), "core", 1)]
    return place(out, quad)


def solution(mesh):
    split = Mesh(mesh.devices.reshape(2, 4, 4, 2, 2), ("zl", "y", "x", "zh", "core"))
    return jax.shard_map(
        local,
        mesh=split,
        in_specs=(P(ROW, COL), P(ROW, COL), P(ROW, COL), P()),
        out_specs=P(ROW, COL),
        check_vma=False,
    )
```

```python
import functools

import jax
import jax.numpy as jnp
from jax import lax
from jax.experimental import pallas as pl
from jax.experimental.pallas import tpu as pltpu
from jax.sharding import Mesh
from jax.sharding import PartitionSpec as P

TILE = 1024
RANK = 256
TILE_DEV = 2
COL_DEV = 6
BLOCK = 256
HALF = 512
ROW = ("zl", "y", "x")
COL = ("zh", "core")
UPPER = ((0, 0), (1, 1), (2, 2), (0, 1), (0, 2), (3, 3), (1, 2), (2, 3), (1, 3), (0, 3))
NB = 128
STRIP = 32
F32 = jnp.float32
HIGHEST = lax.Precision.HIGHEST


def shift(value, axis, step):
    devices = lax.axis_size(axis)
    return lax.ppermute(value, axis, [(i, (i + step) % devices) for i in range(devices)])


def dot(a, b, ca, cb, precision=None):
    return lax.dot_general(
        a, b, (((ca,), (cb,)), ((), ())), precision=precision, preferred_element_type=F32
    )


def params():
    return pltpu.CompilerParams(vmem_limit_bytes=48 << 20)


def place_kernel(axis, where_ref, *refs):
    out = refs[-1]
    for k, ref in enumerate(refs[:-1]):
        size = ref.shape[axis]
        part = pl.ds(pl.multiple_of(where_ref[k] * size, size), size)
        if axis == 0:
            out[part, :] = ref[...]
        else:
            out[:, part] = ref[...]


def place(values, where, axis=0):
    shape = list(values[0].shape)
    shape[axis] *= len(values)
    size = shape[0] * shape[1] * values[0].dtype.itemsize
    return pl.pallas_call(
        functools.partial(place_kernel, axis),
        out_shape=jax.ShapeDtypeStruct(shape, values[0].dtype),
        in_specs=[pl.BlockSpec(memory_space=pltpu.SMEM)]
        + [pl.BlockSpec(memory_space=pltpu.VMEM)] * len(values),
        out_specs=pl.BlockSpec(memory_space=pltpu.VMEM),
        compiler_params=params(),
        cost_estimate=pl.CostEstimate(flops=0, bytes_accessed=2 * size, transcendentals=0),
    )(where, *values)


def in_step(*values):
    return lax.optimization_barrier(values)


def quarters(value):
    rows = value.shape[0] // 4
    return [value[k * rows : (k + 1) * rows] for k in range(4)]


def sends(parts, axis):
    return [parts[0]] + [shift(parts[k], axis, k) for k in (1, 2, 3)]


def neighbours(parts, axis):
    return shift(parts[1], axis, 1), shift(parts[3], axis, 3)


def pieces(piece, axis):
    return sends([piece] * 4, axis)


def update_kernel(where_ref, left, right, right_pieces, left_pieces, *refs):
    outs, (pivot_right, pivot_left, total) = refs[:4], refs[4:]
    j = pl.program_id(0)

    @pl.when(j == 0)
    def _():
        total[...] = jnp.zeros_like(total)

    size = left_pieces.shape[1]
    for k in range(left_pieces.shape[0]):
        x, y = where_ref[k], where_ref[16 + k]
        pivot_right[pl.ds(pl.multiple_of((4 * x + y) * size, size), size), :] = right_pieces[k]
        pivot_left[pl.ds(pl.multiple_of((4 * y + x) * size, size), size), :] = left_pieces[k]
    turned = pivot_right[...].T
    for t in range(TILE_DEV):
        rows = slice(t * TILE, (t + 1) * TILE)
        inner = dot(turned, right[rows, :], 1, 0).astype(jnp.bfloat16)
        product = dot(left[rows, :], inner, 1, 1).astype(jnp.bfloat16)
        for h in range(2):
            total[2 * t + h] += dot(product[h * HALF : (h + 1) * HALF], pivot_left[...], 1, 1)

    @pl.when(j == COL_DEV - 1)
    def _():
        for k, out in enumerate(outs):
            out[...] = total[where_ref[32 + k]]


def update(left, right, gathered, where):
    rows, columns = left.shape
    count, size = gathered.shape[:2]
    steps = columns // RANK
    both = pl.BlockSpec((rows, RANK), lambda j, s: (0, j))
    return pl.pallas_call(
        update_kernel,
        out_shape=[jax.ShapeDtypeStruct((HALF, TILE), F32)] * 4,
        grid_spec=pltpu.PrefetchScalarGridSpec(
            num_scalar_prefetch=1,
            grid=(steps,),
            in_specs=[
                both,
                both,
                pl.BlockSpec((count, size, RANK), lambda j, s: (0, 0, j)),
                pl.BlockSpec((count, size, RANK), lambda j, s: (0, 0, j + steps)),
            ],
            out_specs=[pl.BlockSpec((HALF, TILE), lambda j, s: (0, 0))] * 4,
            scratch_shapes=[pltpu.VMEM((TILE, RANK), jnp.bfloat16)] * 2
            + [pltpu.VMEM((4, HALF, TILE), F32)],
        ),
        compiler_params=params(),
        cost_estimate=pl.CostEstimate(
            flops=12 * rows * columns * RANK, bytes_accessed=8 * rows * columns, transcendentals=0
        ),
    )(where, left, right, gathered, gathered)


def pivot_kernel(where_ref, left, right, panel, out, total):
    j = pl.program_id(0)

    @pl.when(j == 0)
    def _():
        total[...] = jnp.zeros_like(total)
        start = pl.multiple_of(where_ref[1] * BLOCK, BLOCK)
        total[:, pl.ds(start, BLOCK)] = panel[...]

    inner = dot(right[...], right[...], 0, 0).astype(jnp.bfloat16)
    product = dot(left[...], inner, 1, 0).astype(jnp.bfloat16)
    total[...] -= dot(product, left[...], 1, 1)

    @pl.when(j == COL_DEV - 1)
    def _():
        core = where_ref[2]
        for b, (r, c) in enumerate(UPPER):
            above = total[r * BLOCK : (r + 1) * BLOCK, c * BLOCK : (c + 1) * BLOCK]
            below = total[c * BLOCK : (c + 1) * BLOCK, r * BLOCK : (r + 1) * BLOCK]
            out[jnp.where(core == b // 5, 0, 1), b % 5] = (above + below.T) * 0.5


def pivot_update(left, right, panel, slot, my_col, core):
    tile = pl.BlockSpec((TILE, RANK), lambda j, s: (s[0], j))
    return pl.pallas_call(
        pivot_kernel,
        out_shape=jax.ShapeDtypeStruct((2, 5, BLOCK, BLOCK), F32),
        grid_spec=pltpu.PrefetchScalarGridSpec(
            num_scalar_prefetch=1,
            grid=(COL_DEV,),
            in_specs=[tile, tile, pl.BlockSpec((TILE, BLOCK), lambda j, s: (s[0], 0))],
            out_specs=pl.BlockSpec((2, 5, BLOCK, BLOCK), lambda j, s: (0, 0, 0, 0)),
            scratch_shapes=[pltpu.VMEM((TILE, TILE), F32)],
        ),
        compiler_params=params(),
        cost_estimate=pl.CostEstimate(
            flops=10**6, bytes_accessed=10**4, transcendentals=0
        ),
    )(jnp.stack([slot, my_col, core]), left, right, panel)


def factor_kernel(where_ref, mine, other, factor_out, inverse_out, u_ref, x_ref, m_ref, f_ref):
    for b, (r, c) in enumerate(UPPER):
        block = jnp.where(where_ref[0] == b // 5, mine[b % 5], other[b % 5])
        u_ref[r * BLOCK : (r + 1) * BLOCK, c * BLOCK : (c + 1) * BLOCK] = block
    x_ref[...] = jnp.zeros_like(x_ref)
    row = lax.broadcasted_iota(jnp.int32, (NB, NB), 0)
    column = lax.broadcasted_iota(jnp.int32, (NB, NB), 1)
    strip_row = lax.broadcasted_iota(jnp.int32, (STRIP, NB), 0)
    for k in range(TILE // NB):
        k0, k1 = k * NB, (k + 1) * NB
        m_ref[:, :NB] = u_ref[k0:k1, k0:k1]
        m_ref[:, NB:] = jnp.where(row == column, 1.0, 0.0).astype(F32)

        def strip(t, carry):
            start = pl.multiple_of(t * STRIP, STRIP)
            ps = m_ref[pl.ds(start, STRIP), :NB]
            pi = m_ref[pl.ds(start, STRIP), NB:]
            turned = pltpu.roll(ps, NB - start, 1)
            c = [jnp.broadcast_to(turned[:, j : j + 1], (STRIP, NB)) for j in range(STRIP)]
            for j in range(STRIP):
                inv = lax.rsqrt(jnp.broadcast_to(c[j][j : j + 1, :], (STRIP, NB)))
                col = c[j] * inv
                for q in range(j + 1, STRIP):
                    c[q] = c[q] - col * jnp.broadcast_to(col[q : q + 1, :], (STRIP, NB))
                us = jnp.broadcast_to(ps[j : j + 1, :], (STRIP, NB)) * inv
                ui = jnp.broadcast_to(pi[j : j + 1, :], (STRIP, NB)) * inv
                below = jnp.where(strip_row > j, col, 0.0)
                ps = jnp.where(strip_row == j, us, ps - below * us)
                pi = jnp.where(strip_row == j, ui, pi - below * ui)
            f_ref[pl.ds(start, STRIP), :NB] = ps
            f_ref[pl.ds(start, STRIP), NB:] = pi
            m_ref[:, :NB] -= dot(ps, ps, 0, 0, HIGHEST)
            m_ref[:, NB:] -= dot(ps, pi, 0, 0, HIGHEST)
            return carry

        lax.fori_loop(0, NB // STRIP, strip, 0)
        xk = f_ref[:, NB:]
        u_ref[k0:k1, k0:k1] = f_ref[:, :NB]
        if k:
            x_ref[k0:k1, :k0] = dot(xk, x_ref[k0:k1, :k0], 1, 0, HIGHEST)
        x_ref[k0:k1, k0:k1] = xk
        if k1 < TILE:
            w = dot(xk, u_ref[k0:k1, k1:], 1, 0, HIGHEST)
            u_ref[k0:k1, k1:] = w
            for i in range(k + 1, TILE // NB):
                wi = w[:, i * NB - k1 : (i + 1) * NB - k1]
                u_ref[i * NB : (i + 1) * NB, i * NB :] -= dot(
                    wi, w[:, i * NB - k1 :], 0, 0, HIGHEST
                )
                x_ref[i * NB : (i + 1) * NB, :k1] -= dot(wi, x_ref[k0:k1, :k1], 0, 0, HIGHEST)
    inverse_out[...] = x_ref[...]
    first = pl.multiple_of(where_ref[0] * HALF, HALF)
    for b in range(4):
        block = u_ref[b * BLOCK : (b + 1) * BLOCK, pl.ds(first, HALF)].T
        r = lax.broadcasted_iota(jnp.int32, (HALF, BLOCK), 0) + first
        c = lax.broadcasted_iota(jnp.int32, (HALF, BLOCK), 1) + b * BLOCK
        factor_out[:, b * BLOCK : (b + 1) * BLOCK] = jnp.where(r >= c, block, 0.0)


def factor_and_inverse(mine, other, core):
    return pl.pallas_call(
        factor_kernel,
        out_shape=(
            jax.ShapeDtypeStruct((HALF, TILE), F32),
            jax.ShapeDtypeStruct((TILE, TILE), F32),
        ),
        in_specs=[pl.BlockSpec(memory_space=pltpu.SMEM)]
        + [pl.BlockSpec(memory_space=pltpu.VMEM)] * 2,
        out_specs=[pl.BlockSpec(memory_space=pltpu.VMEM)] * 2,
        scratch_shapes=[pltpu.VMEM((TILE, TILE), F32)] * 2 + [pltpu.VMEM((NB, 2 * NB), F32)] * 2,
        compiler_params=params(),
        cost_estimate=pl.CostEstimate(
            flops=10**9, bytes_accessed=5 * 2**20, transcendentals=0
        ),
    )(core.reshape(1), mine, other)


def local(panel_tiles, left_u, earlier_right_factors, tile_global_index):
    tile_count = tile_global_index.shape[0]
    pivot_position = jnp.sum(
        jnp.where(tile_global_index == 0, jnp.arange(tile_count, dtype=jnp.int32), 0)
    )
    owner = pivot_position >> 1
    slot = pivot_position & 1
    away = {
        "x": (lax.axis_index("x") - owner) & 3,
        "y": (lax.axis_index("y") - (owner >> 2)) & 3,
        "zl": (lax.axis_index("zl") - (owner >> 4)) & 1,
    }
    zh, core = lax.axis_index("zh"), lax.axis_index("core")
    my_col = lax.axis_index(COL)

    def slot_quarters(value):
        return [
            lax.dynamic_slice_in_dim(value, slot * TILE + k * BLOCK, BLOCK, 0) for k in range(4)
        ]

    where = {a: jnp.stack([(away[a] - k) & 3 for k in range(4)]) for a in ("x", "y")}
    quad = jnp.stack([2 * zh + core, 2 * zh + 1 - core, 2 - 2 * zh + core, 3 - 2 * zh - core])
    square = jnp.arange(16, dtype=jnp.int32)
    sixteen = jnp.concatenate([(square - owner) & 3, ((square >> 2) - (owner >> 2)) & 3, quad[::-1]])
    holds = away["zl"] == 0

    def slot_quarters(value):
        return [
            lax.dynamic_slice_in_dim(value, slot * TILE + k * BLOCK, BLOCK, 0) for k in range(4)
        ]

    v, u = slot_quarters(earlier_right_factors), slot_quarters(left_u)
    *u, slot = in_step(*u, slot)
    v1, v3 = neighbours(v, "x")
    u1, u3 = neighbours(u, "y")
    upper = pivot_update(left_u, earlier_right_factors, panel_tiles, slot, my_col, core)
    s = upper[0] + shift(upper[1], "core", 1)
    v2, u2, v1, v3, u1, u3, _ = in_step(v[2], u[2], v1, v3, u1, u3, s)
    s = s + shift(s, "zh", 1)
    v = lax.select_n(away["x"], v[0], v1, shift(v2, "x", 2), v3)
    u = lax.select_n(away["y"], u[0], u1, shift(u2, "y", 2), u3)
    v, u, s = in_step(v, u, s)
    v, u = sends(quarters(v), "y"), sends(quarters(u), "x")
    s = lax.select_n(away["x"], *sends(quarters(s.reshape(5 * BLOCK, BLOCK)), "x"))
    v, u, s = in_step(lax.select_n(away["y"], *v), lax.select_n(away["x"], *u), s)
    v = jnp.where(holds, v, shift(v, "zl", 1))
    u = jnp.where(holds, u, shift(u, "zl", 1))
    gathered = lax.all_gather(jnp.concatenate([v, u], axis=1), ("y", "x"))

    s = lax.select_n(away["y"], *sends(quarters(s), "y"))
    s = jnp.where(holds, s, shift(s, "zl", 1))
    s = place(pieces(s, "y"), where["y"])
    mine = place(pieces(s, "x"), where["x"]).reshape(5, BLOCK, BLOCK)
    other = shift(mine, "core", 1)

    tiles = [lax.dynamic_slice_in_dim(panel_tiles, z * TILE, TILE, 0) for z in (zh, 1 - zh)]
    tiles = [tiles[0], shift(tiles[1], "zh", 1)]
    own = [lax.dynamic_slice_in_dim(t, core * HALF, HALF, 0) for t in tiles]
    sent = [lax.dynamic_slice_in_dim(t, (1 - core) * HALF, HALF, 0) for t in tiles]
    sent = [shift(t, "core", 1) for t in sent]
    panel_rows = place([own[0], sent[0], own[1], sent[1]], quad, 1)

    gathered, mine, other, panel_rows = in_step(gathered, mine, other, panel_rows)
    far_other, far, near_other, near = update(left_u, earlier_right_factors, gathered, sixteen)
    far = far + shift(far_other, "core", 1)
    near = near + shift(near_other, "core", 1)
    far, mine, other = in_step(far, mine, other)
    far = shift(far, "zh", 1)
    factor_rows, inverse = factor_and_inverse(mine, other, core)
    updated = panel_rows - near - far

    chosen = jnp.logical_and(lax.axis_index(ROW) == owner, slot == zh)

    def solved(z):
        inv = lax.dynamic_slice_in_dim(inverse, z * HALF, HALF, 0)
        fac = lax.dynamic_slice_in_dim(factor_rows, z * HALF, HALF, 1)
        return jnp.where(chosen, fac, dot(updated, inv, 1, 1, lax.Precision.HIGH))

    def column(value, c):
        return lax.dynamic_slice_in_dim(value, c * BLOCK, BLOCK, 1)

    out_far = shift(solved(1 - zh), "zh", 1)
    out_near = solved(zh)
    out = [column(out_near, core), shift(column(out_near, 1 - core), "core", 1)]
    out += [column(out_far, core), shift(column(out_far, 1 - core), "core", 1)]
    return place(out, quad)


def solution(mesh):
    split = Mesh(mesh.devices.reshape(2, 4, 4, 2, 2), ("zl", "y", "x", "zh", "core"))
    return jax.shard_map(
        local,
        mesh=split,
        in_specs=(P(ROW, COL), P(ROW, COL), P(ROW, COL), P()),
        out_specs=P(ROW, COL),
        check_vma=False,
    )
```

```python
import functools

import jax
import jax.numpy as jnp
from jax import lax
from jax.experimental import pallas as pl
from jax.experimental.pallas import tpu as pltpu
from jax.sharding import Mesh
from jax.sharding import PartitionSpec as P

TILE = 1024
RANK = 256
TILE_DEV = 2
COL_DEV = 6
BLOCK = 256
HALF = 512
ROW = ("zl", "y", "x")
COL = ("zh", "core")
UPPER = ((0, 0), (1, 1), (2, 2), (0, 1), (0, 2), (3, 3), (1, 2), (2, 3), (1, 3), (0, 3))
NB = 128
STRIP = 32
F32 = jnp.float32
HIGHEST = lax.Precision.HIGHEST


def shift(value, axis, step):
    devices = lax.axis_size(axis)
    return lax.ppermute(value, axis, [(i, (i + step) % devices) for i in range(devices)])


def dot(a, b, ca, cb, precision=None):
    return lax.dot_general(
        a, b, (((ca,), (cb,)), ((), ())), precision=precision, preferred_element_type=F32
    )


def params():
    return pltpu.CompilerParams(vmem_limit_bytes=48 << 20)


def place_kernel(axis, where_ref, *refs):
    out = refs[-1]
    for k, ref in enumerate(refs[:-1]):
        size = ref.shape[axis]
        part = pl.ds(pl.multiple_of(where_ref[k] * size, size), size)
        if axis == 0:
            out[part, :] = ref[...]
        else:
            out[:, part] = ref[...]


def place(values, where, axis=0):
    shape = list(values[0].shape)
    shape[axis] *= len(values)
    size = shape[0] * shape[1] * values[0].dtype.itemsize
    return pl.pallas_call(
        functools.partial(place_kernel, axis),
        out_shape=jax.ShapeDtypeStruct(shape, values[0].dtype),
        in_specs=[pl.BlockSpec(memory_space=pltpu.SMEM)]
        + [pl.BlockSpec(memory_space=pltpu.VMEM)] * len(values),
        out_specs=pl.BlockSpec(memory_space=pltpu.VMEM),
        compiler_params=params(),
        cost_estimate=pl.CostEstimate(flops=0, bytes_accessed=2 * size, transcendentals=0),
    )(where, *values)


def in_step(*values):
    return lax.optimization_barrier(values)


def quarters(value):
    rows = value.shape[0] // 4
    return [value[k * rows : (k + 1) * rows] for k in range(4)]


def sends(parts, axis):
    return [parts[0]] + [shift(parts[k], axis, k) for k in (1, 2, 3)]


def neighbours(parts, axis):
    return shift(parts[1], axis, 1), shift(parts[3], axis, 3)


def pieces(piece, axis):
    return sends([piece] * 4, axis)


def update_kernel(where_ref, left, right, right_pieces, left_pieces, *refs):
    outs, (pivot_right, pivot_left, total) = refs[:4], refs[4:]
    j = pl.program_id(0)

    @pl.when(j == 0)
    def _():
        total[...] = jnp.zeros_like(total)

    size = left_pieces.shape[1]
    for k in range(left_pieces.shape[0]):
        x, y = where_ref[k], where_ref[16 + k]
        pivot_right[pl.ds(pl.multiple_of((4 * x + y) * size, size), size), :] = right_pieces[k]
        pivot_left[pl.ds(pl.multiple_of((4 * y + x) * size, size), size), :] = left_pieces[k]
    turned = pivot_right[...].T
    for t in range(TILE_DEV):
        rows = slice(t * TILE, (t + 1) * TILE)
        inner = dot(turned, right[rows, :], 1, 0).astype(jnp.bfloat16)
        product = dot(left[rows, :], inner, 1, 1).astype(jnp.bfloat16)
        for h in range(2):
            total[2 * t + h] += dot(product[h * HALF : (h + 1) * HALF], pivot_left[...], 1, 1)

    @pl.when(j == COL_DEV - 1)
    def _():
        for k, out in enumerate(outs):
            out[...] = total[where_ref[32 + k]]


def update(left, right, gathered, where):
    rows, columns = left.shape
    count, size = gathered.shape[:2]
    steps = columns // RANK
    both = pl.BlockSpec((rows, RANK), lambda j, s: (0, j))
    return pl.pallas_call(
        update_kernel,
        out_shape=[jax.ShapeDtypeStruct((HALF, TILE), F32)] * 4,
        grid_spec=pltpu.PrefetchScalarGridSpec(
            num_scalar_prefetch=1,
            grid=(steps,),
            in_specs=[
                both,
                both,
                pl.BlockSpec((count, size, RANK), lambda j, s: (0, 0, j)),
                pl.BlockSpec((count, size, RANK), lambda j, s: (0, 0, j + steps)),
            ],
            out_specs=[pl.BlockSpec((HALF, TILE), lambda j, s: (0, 0))] * 4,
            scratch_shapes=[pltpu.VMEM((TILE, RANK), jnp.bfloat16)] * 2
            + [pltpu.VMEM((4, HALF, TILE), F32)],
        ),
        compiler_params=params(),
        cost_estimate=pl.CostEstimate(
            flops=12 * rows * columns * RANK, bytes_accessed=8 * rows * columns, transcendentals=0
        ),
    )(where, left, right, gathered, gathered)


def pivot_kernel(where_ref, left, right, panel, out, total):
    j = pl.program_id(0)

    @pl.when(j == 0)
    def _():
        total[...] = jnp.zeros_like(total)
        start = pl.multiple_of(where_ref[1] * BLOCK, BLOCK)
        total[:, pl.ds(start, BLOCK)] = panel[...]

    inner = dot(right[...], right[...], 0, 0).astype(jnp.bfloat16)
    product = dot(left[...], inner, 1, 0).astype(jnp.bfloat16)
    total[...] -= dot(product, left[...], 1, 1)

    @pl.when(j == COL_DEV - 1)
    def _():
        core = where_ref[2]
        for b, (r, c) in enumerate(UPPER):
            above = total[r * BLOCK : (r + 1) * BLOCK, c * BLOCK : (c + 1) * BLOCK]
            below = total[c * BLOCK : (c + 1) * BLOCK, r * BLOCK : (r + 1) * BLOCK]
            out[jnp.where(core == b // 5, 0, 1), b % 5] = (above + below.T) * 0.5


def pivot_update(left, right, panel, slot, my_col, core):
    tile = pl.BlockSpec((TILE, RANK), lambda j, s: (s[0], j))
    return pl.pallas_call(
        pivot_kernel,
        out_shape=jax.ShapeDtypeStruct((2, 5, BLOCK, BLOCK), F32),
        grid_spec=pltpu.PrefetchScalarGridSpec(
            num_scalar_prefetch=1,
            grid=(COL_DEV,),
            in_specs=[tile, tile, pl.BlockSpec((TILE, BLOCK), lambda j, s: (s[0], 0))],
            out_specs=pl.BlockSpec((2, 5, BLOCK, BLOCK), lambda j, s: (0, 0, 0, 0)),
            scratch_shapes=[pltpu.VMEM((TILE, TILE), F32)],
        ),
        compiler_params=params(),
        cost_estimate=pl.CostEstimate(
            flops=10**6, bytes_accessed=10**4, transcendentals=0
        ),
    )(jnp.stack([slot, my_col, core]), left, right, panel)


def factor_kernel(where_ref, mine, other, factor_out, inverse_out, u_ref, x_ref, m_ref, f_ref):
    for b, (r, c) in enumerate(UPPER):
        block = jnp.where(where_ref[0] == b // 5, mine[b % 5], other[b % 5])
        u_ref[r * BLOCK : (r + 1) * BLOCK, c * BLOCK : (c + 1) * BLOCK] = block
    x_ref[...] = jnp.zeros_like(x_ref)
    row = lax.broadcasted_iota(jnp.int32, (NB, NB), 0)
    column = lax.broadcasted_iota(jnp.int32, (NB, NB), 1)
    strip_row = lax.broadcasted_iota(jnp.int32, (STRIP, NB), 0)
    for k in range(TILE // NB):
        k0, k1 = k * NB, (k + 1) * NB
        m_ref[:, :NB] = u_ref[k0:k1, k0:k1]
        m_ref[:, NB:] = jnp.where(row == column, 1.0, 0.0).astype(F32)

        def strip(t, carry):
            start = pl.multiple_of(t * STRIP, STRIP)
            ps = m_ref[pl.ds(start, STRIP), :NB]
            pi = m_ref[pl.ds(start, STRIP), NB:]
            turned = pltpu.roll(ps, NB - start, 1)
            c = [jnp.broadcast_to(turned[:, j : j + 1], (STRIP, NB)) for j in range(STRIP)]
            for j in range(STRIP):
                inv = lax.rsqrt(jnp.broadcast_to(c[j][j : j + 1, :], (STRIP, NB)))
                col = c[j] * inv
                for q in range(j + 1, STRIP):
                    c[q] = c[q] - col * jnp.broadcast_to(col[q : q + 1, :], (STRIP, NB))
                us = jnp.broadcast_to(ps[j : j + 1, :], (STRIP, NB)) * inv
                ui = jnp.broadcast_to(pi[j : j + 1, :], (STRIP, NB)) * inv
                below = jnp.where(strip_row > j, col, 0.0)
                ps = jnp.where(strip_row == j, us, ps - below * us)
                pi = jnp.where(strip_row == j, ui, pi - below * ui)
            f_ref[pl.ds(start, STRIP), :NB] = ps
            f_ref[pl.ds(start, STRIP), NB:] = pi

            @pl.when(t < NB // STRIP - 1)
            def _():
                m_ref[:, :NB] -= dot(ps, ps, 0, 0, HIGHEST)
                m_ref[:, NB:] -= dot(ps, pi, 0, 0, HIGHEST)

            return carry

        lax.fori_loop(0, NB // STRIP, strip, 0)
        xk = f_ref[:, NB:]
        u_ref[k0:k1, k0:k1] = f_ref[:, :NB]
        if k:
            x_ref[k0:k1, :k0] = dot(xk, x_ref[k0:k1, :k0], 1, 0, HIGHEST)
        x_ref[k0:k1, k0:k1] = xk
        if k1 < TILE:
            w = dot(xk, u_ref[k0:k1, k1:], 1, 0, HIGHEST)
            u_ref[k0:k1, k1:] = w
            for i in range(k + 1, TILE // NB):
                wi = w[:, i * NB - k1 : (i + 1) * NB - k1]
                u_ref[i * NB : (i + 1) * NB, i * NB :] -= dot(
                    wi, w[:, i * NB - k1 :], 0, 0, HIGHEST
                )
                x_ref[i * NB : (i + 1) * NB, :k1] -= dot(wi, x_ref[k0:k1, :k1], 0, 0, HIGHEST)
    inverse_out[...] = x_ref[...]
    first = pl.multiple_of(where_ref[0] * HALF, HALF)
    for b in range(4):
        block = u_ref[b * BLOCK : (b + 1) * BLOCK, pl.ds(first, HALF)].T
        r = lax.broadcasted_iota(jnp.int32, (HALF, BLOCK), 0) + first
        c = lax.broadcasted_iota(jnp.int32, (HALF, BLOCK), 1) + b * BLOCK
        factor_out[:, b * BLOCK : (b + 1) * BLOCK] = jnp.where(r >= c, block, 0.0)


def factor_and_inverse(mine, other, core):
    return pl.pallas_call(
        factor_kernel,
        out_shape=(
            jax.ShapeDtypeStruct((HALF, TILE), F32),
            jax.ShapeDtypeStruct((TILE, TILE), F32),
        ),
        in_specs=[pl.BlockSpec(memory_space=pltpu.SMEM)]
        + [pl.BlockSpec(memory_space=pltpu.VMEM)] * 2,
        out_specs=[pl.BlockSpec(memory_space=pltpu.VMEM)] * 2,
        scratch_shapes=[pltpu.VMEM((TILE, TILE), F32)] * 2 + [pltpu.VMEM((NB, 2 * NB), F32)] * 2,
        compiler_params=params(),
        cost_estimate=pl.CostEstimate(
            flops=10**9, bytes_accessed=5 * 2**20, transcendentals=0
        ),
    )(core.reshape(1), mine, other)


def local(panel_tiles, left_u, earlier_right_factors, tile_global_index):
    tile_count = tile_global_index.shape[0]
    pivot_position = jnp.sum(
        jnp.where(tile_global_index == 0, jnp.arange(tile_count, dtype=jnp.int32), 0)
    )
    owner = pivot_position >> 1
    slot = pivot_position & 1
    away = {
        "x": (lax.axis_index("x") - owner) & 3,
        "y": (lax.axis_index("y") - (owner >> 2)) & 3,
        "zl": (lax.axis_index("zl") - (owner >> 4)) & 1,
    }
    zh, core = lax.axis_index("zh"), lax.axis_index("core")
    my_col = lax.axis_index(COL)

    def slot_quarters(value):
        return [
            lax.dynamic_slice_in_dim(value, slot * TILE + k * BLOCK, BLOCK, 0) for k in range(4)
        ]

    where = {a: jnp.stack([(away[a] - k) & 3 for k in range(4)]) for a in ("x", "y")}
    quad = jnp.stack([2 * zh + core, 2 * zh + 1 - core, 2 - 2 * zh + core, 3 - 2 * zh - core])
    square = jnp.arange(16, dtype=jnp.int32)
    sixteen = jnp.concatenate([(square - owner) & 3, ((square >> 2) - (owner >> 2)) & 3, quad[::-1]])
    holds = away["zl"] == 0

    def slot_quarters(value):
        return [
            lax.dynamic_slice_in_dim(value, slot * TILE + k * BLOCK, BLOCK, 0) for k in range(4)
        ]

    v, u = slot_quarters(earlier_right_factors), slot_quarters(left_u)
    *u, slot = in_step(*u, slot)
    v1, v3 = neighbours(v, "x")
    u1, u3 = neighbours(u, "y")
    upper = pivot_update(left_u, earlier_right_factors, panel_tiles, slot, my_col, core)
    s = upper[0] + shift(upper[1], "core", 1)
    v2, u2, v1, v3, u1, u3, _ = in_step(v[2], u[2], v1, v3, u1, u3, s)
    s = (s + shift(s, "zh", 1)).reshape(5 * BLOCK, BLOCK)
    v = lax.select_n(away["x"], v[0], v1, shift(v2, "x", 2), v3)
    u = lax.select_n(away["y"], u[0], u1, shift(u2, "y", 2), u3)
    v, u = in_step(v, u)
    v, u = sends(quarters(v), "y"), sends(quarters(u), "x")
    v, u, s = in_step(lax.select_n(away["y"], *v), lax.select_n(away["x"], *u), s)
    v = jnp.where(holds, v, shift(v, "zl", 1))
    u = jnp.where(holds, u, shift(u, "zl", 1))
    gathered = lax.all_gather(jnp.concatenate([v, u], axis=1), ("y", "x"))

    s = lax.select_n(away["x"], *sends(quarters(s), "x"))
    s = lax.select_n(away["y"], *sends(quarters(s), "y"))
    s = jnp.where(holds, s, shift(s, "zl", 1))
    s = place(pieces(s, "y"), where["y"])
    mine = place(pieces(s, "x"), where["x"]).reshape(5, BLOCK, BLOCK)
    other = shift(mine, "core", 1)

    tiles = [lax.dynamic_slice_in_dim(panel_tiles, z * TILE, TILE, 0) for z in (zh, 1 - zh)]
    tiles = [tiles[0], shift(tiles[1], "zh", 1)]
    own = [lax.dynamic_slice_in_dim(t, core * HALF, HALF, 0) for t in tiles]
    sent = [lax.dynamic_slice_in_dim(t, (1 - core) * HALF, HALF, 0) for t in tiles]
    sent = [shift(t, "core", 1) for t in sent]
    panel_rows = place([own[0], sent[0], own[1], sent[1]], quad, 1)

    gathered, mine, other, panel_rows = in_step(gathered, mine, other, panel_rows)
    far_other, far, near_other, near = update(left_u, earlier_right_factors, gathered, sixteen)
    far = far + shift(far_other, "core", 1)
    near = near + shift(near_other, "core", 1)
    far, near, mine, other = in_step(far, panel_rows - near, mine, other)
    far = shift(far, "zh", 1)
    factor_rows, inverse = factor_and_inverse(mine, other, core)
    updated = near - far

    chosen = jnp.logical_and(lax.axis_index(ROW) == owner, slot == zh)

    def solved(z):
        inv = lax.dynamic_slice_in_dim(inverse, z * HALF, HALF, 0)
        fac = lax.dynamic_slice_in_dim(factor_rows, z * HALF, HALF, 1)
        return jnp.where(chosen, fac, dot(updated, inv, 1, 1, lax.Precision.HIGH))

    def column(value, c):
        return lax.dynamic_slice_in_dim(value, c * BLOCK, BLOCK, 1)

    out_far = shift(solved(1 - zh), "zh", 1)
    out_near = solved(zh)
    out = [column(out_near, core), shift(column(out_near, 1 - core), "core", 1)]
    out += [column(out_far, core), shift(column(out_far, 1 - core), "core", 1)]
    return place(out, quad)


def solution(mesh):
    split = Mesh(mesh.devices.reshape(2, 4, 4, 2, 2), ("zl", "y", "x", "zh", "core"))
    return jax.shard_map(
        local,
        mesh=split,
        in_specs=(P(ROW, COL), P(ROW, COL), P(ROW, COL), P()),
        out_specs=P(ROW, COL),
        check_vma=False,
    )
```

```python
import functools

import jax
import jax.numpy as jnp
from jax import lax
from jax.experimental import pallas as pl
from jax.experimental.pallas import tpu as pltpu
from jax.sharding import Mesh
from jax.sharding import PartitionSpec as P

TILE = 1024
RANK = 256
TILE_DEV = 2
COL_DEV = 6
BLOCK = 256
HALF = 512
ROW = ("zl", "y", "x")
COL = ("zh", "core")
UPPER = ((0, 0), (1, 1), (2, 2), (0, 1), (0, 2), (3, 3), (1, 2), (2, 3), (1, 3), (0, 3))
NB = 128
STRIP = 32
F32 = jnp.float32
HIGHEST = lax.Precision.HIGHEST


def shift(value, axis, step):
    devices = lax.axis_size(axis)
    return lax.ppermute(value, axis, [(i, (i + step) % devices) for i in range(devices)])


def dot(a, b, ca, cb, precision=None):
    return lax.dot_general(
        a, b, (((ca,), (cb,)), ((), ())), precision=precision, preferred_element_type=F32
    )


def params():
    return pltpu.CompilerParams(vmem_limit_bytes=48 << 20)


def place_kernel(axis, where_ref, *refs):
    out = refs[-1]
    for k, ref in enumerate(refs[:-1]):
        size = ref.shape[axis]
        part = pl.ds(pl.multiple_of(where_ref[k] * size, size), size)
        if axis == 0:
            out[part, :] = ref[...]
        else:
            out[:, part] = ref[...]


def place(values, where, axis=0):
    shape = list(values[0].shape)
    shape[axis] *= len(values)
    size = shape[0] * shape[1] * values[0].dtype.itemsize
    return pl.pallas_call(
        functools.partial(place_kernel, axis),
        out_shape=jax.ShapeDtypeStruct(shape, values[0].dtype),
        in_specs=[pl.BlockSpec(memory_space=pltpu.SMEM)]
        + [pl.BlockSpec(memory_space=pltpu.VMEM)] * len(values),
        out_specs=pl.BlockSpec(memory_space=pltpu.VMEM),
        compiler_params=params(),
        cost_estimate=pl.CostEstimate(flops=0, bytes_accessed=2 * size, transcendentals=0),
    )(where, *values)


def in_step(*values):
    return lax.optimization_barrier(values)


def quarters(value):
    rows = value.shape[0] // 4
    return [value[k * rows : (k + 1) * rows] for k in range(4)]


def sends(parts, axis):
    return [parts[0]] + [shift(parts[k], axis, k) for k in (1, 2, 3)]


def neighbours(parts, axis):
    return shift(parts[1], axis, 1), shift(parts[3], axis, 3)


def pieces(piece, axis):
    return sends([piece] * 4, axis)


def update_kernel(where_ref, left, right, right_pieces, left_pieces, *refs):
    outs, (pivot_right, pivot_left, total) = refs[:4], refs[4:]
    j = pl.program_id(0)

    @pl.when(j == 0)
    def _():
        total[...] = jnp.zeros_like(total)

    size = left_pieces.shape[1]
    for k in range(left_pieces.shape[0]):
        x, y = where_ref[k], where_ref[16 + k]
        pivot_right[pl.ds(pl.multiple_of((4 * x + y) * size, size), size), :] = right_pieces[k]
        pivot_left[pl.ds(pl.multiple_of((4 * y + x) * size, size), size), :] = left_pieces[k]
    turned = pivot_right[...].T
    for t in range(TILE_DEV):
        rows = slice(t * TILE, (t + 1) * TILE)
        inner = dot(turned, right[rows, :], 1, 0).astype(jnp.bfloat16)
        product = dot(left[rows, :], inner, 1, 1).astype(jnp.bfloat16)
        for h in range(2):
            total[2 * t + h] += dot(product[h * HALF : (h + 1) * HALF], pivot_left[...], 1, 1)

    @pl.when(j == COL_DEV - 1)
    def _():
        for k, out in enumerate(outs):
            out[...] = total[where_ref[32 + k]]


def update(left, right, gathered, where):
    rows, columns = left.shape
    count, size = gathered.shape[:2]
    steps = columns // RANK
    both = pl.BlockSpec((rows, RANK), lambda j, s: (0, j))
    return pl.pallas_call(
        update_kernel,
        out_shape=[jax.ShapeDtypeStruct((HALF, TILE), F32)] * 4,
        grid_spec=pltpu.PrefetchScalarGridSpec(
            num_scalar_prefetch=1,
            grid=(steps,),
            in_specs=[
                both,
                both,
                pl.BlockSpec((count, size, RANK), lambda j, s: (0, 0, j)),
                pl.BlockSpec((count, size, RANK), lambda j, s: (0, 0, j + steps)),
            ],
            out_specs=[pl.BlockSpec((HALF, TILE), lambda j, s: (0, 0))] * 4,
            scratch_shapes=[pltpu.VMEM((TILE, RANK), jnp.bfloat16)] * 2
            + [pltpu.VMEM((4, HALF, TILE), F32)],
        ),
        compiler_params=params(),
        cost_estimate=pl.CostEstimate(
            flops=12 * rows * columns * RANK, bytes_accessed=8 * rows * columns, transcendentals=0
        ),
    )(where, left, right, gathered, gathered)


def pivot_kernel(where_ref, left, right, panel, out, total):
    j = pl.program_id(0)

    @pl.when(j == 0)
    def _():
        total[...] = jnp.zeros_like(total)
        start = pl.multiple_of(where_ref[1] * BLOCK, BLOCK)
        total[:, pl.ds(start, BLOCK)] = panel[...]

    inner = dot(right[...], right[...], 0, 0).astype(jnp.bfloat16)
    product = dot(left[...], inner, 1, 0).astype(jnp.bfloat16)
    total[...] -= dot(product, left[...], 1, 1)

    @pl.when(j == COL_DEV - 1)
    def _():
        core = where_ref[2]
        for b, (r, c) in enumerate(UPPER):
            above = total[r * BLOCK : (r + 1) * BLOCK, c * BLOCK : (c + 1) * BLOCK]
            below = total[c * BLOCK : (c + 1) * BLOCK, r * BLOCK : (r + 1) * BLOCK]
            out[jnp.where(core == b // 5, 0, 1), b % 5] = (above + below.T) * 0.5


def pivot_update(left, right, panel, slot, my_col, core):
    tile = pl.BlockSpec((TILE, RANK), lambda j, s: (s[0], j))
    return pl.pallas_call(
        pivot_kernel,
        out_shape=jax.ShapeDtypeStruct((2, 5, BLOCK, BLOCK), F32),
        grid_spec=pltpu.PrefetchScalarGridSpec(
            num_scalar_prefetch=1,
            grid=(COL_DEV,),
            in_specs=[tile, tile, pl.BlockSpec((TILE, BLOCK), lambda j, s: (s[0], 0))],
            out_specs=pl.BlockSpec((2, 5, BLOCK, BLOCK), lambda j, s: (0, 0, 0, 0)),
            scratch_shapes=[pltpu.VMEM((TILE, TILE), F32)],
        ),
        compiler_params=params(),
        cost_estimate=pl.CostEstimate(
            flops=10**6, bytes_accessed=10**4, transcendentals=0
        ),
    )(jnp.stack([slot, my_col, core]), left, right, panel)


def factor_kernel(where_ref, mine, other, factor_out, inverse_out, u_ref, x_ref, m_ref, f_ref, w_ref):
    for b, (r, c) in enumerate(UPPER):
        block = jnp.where(where_ref[0] == b // 5, mine[b % 5], other[b % 5])
        u_ref[r * BLOCK : (r + 1) * BLOCK, c * BLOCK : (c + 1) * BLOCK] = block
    x_ref[...] = jnp.zeros_like(x_ref)
    row = lax.broadcasted_iota(jnp.int32, (NB, NB), 0)
    column = lax.broadcasted_iota(jnp.int32, (NB, NB), 1)
    strip_row = lax.broadcasted_iota(jnp.int32, (STRIP, NB), 0)
    for k in range(TILE // NB):
        k0, k1 = k * NB, (k + 1) * NB
        m_ref[:, :NB] = u_ref[k0:k1, k0:k1]
        m_ref[:, NB:] = jnp.where(row == column, 1.0, 0.0).astype(F32)

        def strip(t, carry):
            start = pl.multiple_of(t * STRIP, STRIP)
            if k and k1 < TILE:
                size = (TILE - k1) // (NB // STRIP)
                wt = w_ref[pl.ds(pl.multiple_of(t * size, size), size), :]
                rows = pl.ds(pl.multiple_of(k1 + t * size, STRIP), size)
                u_ref[rows, k1:] -= dot(wt, u_ref[k0 - NB : k0, k1:], 1, 0, HIGHEST)
                x_ref[rows, :k0] -= dot(wt, x_ref[k0 - NB : k0, :k0], 1, 0, HIGHEST)
            ps = m_ref[pl.ds(start, STRIP), :NB]
            pi = m_ref[pl.ds(start, STRIP), NB:]
            turned = pltpu.roll(ps, NB - start, 1)
            c = [jnp.broadcast_to(turned[:, j : j + 1], (STRIP, NB)) for j in range(STRIP)]
            for j in range(STRIP):
                inv = lax.rsqrt(jnp.broadcast_to(c[j][j : j + 1, :], (STRIP, NB)))
                col = c[j] * inv
                for q in range(j + 1, STRIP):
                    c[q] = c[q] - col * jnp.broadcast_to(col[q : q + 1, :], (STRIP, NB))
                us = jnp.broadcast_to(ps[j : j + 1, :], (STRIP, NB)) * inv
                ui = jnp.broadcast_to(pi[j : j + 1, :], (STRIP, NB)) * inv
                below = jnp.where(strip_row > j, col, 0.0)
                ps = jnp.where(strip_row == j, us, ps - below * us)
                pi = jnp.where(strip_row == j, ui, pi - below * ui)
            f_ref[pl.ds(start, STRIP), :NB] = ps
            f_ref[pl.ds(start, STRIP), NB:] = pi

            @pl.when(t < NB // STRIP - 1)
            def _():
                m_ref[:, :NB] -= dot(ps, ps, 0, 0, HIGHEST)
                m_ref[:, NB:] -= dot(ps, pi, 0, 0, HIGHEST)

            return carry

        lax.fori_loop(0, NB // STRIP, strip, 0)
        xk = f_ref[:, NB:]
        u_ref[k0:k1, k0:k1] = f_ref[:, :NB]
        if k:
            x_ref[k0:k1, :k0] = dot(xk, x_ref[k0:k1, :k0], 1, 0, HIGHEST)
        x_ref[k0:k1, k0:k1] = xk
        if k1 < TILE:
            w = dot(xk, u_ref[k0:k1, k1:], 1, 0, HIGHEST)
            u_ref[k0:k1, k1:] = w
            k2 = k1 + NB
            u_ref[k1:k2, k1:] -= dot(w[:, :NB], w, 0, 0, HIGHEST)
            x_ref[k1:k2, :k1] -= dot(w[:, :NB], x_ref[k0:k1, :k1], 0, 0, HIGHEST)
            if k2 < TILE:
                w_ref[: TILE - k2, :] = w[:, NB:].T
    inverse_out[...] = x_ref[...]
    first = pl.multiple_of(where_ref[0] * HALF, HALF)
    for b in range(4):
        block = u_ref[b * BLOCK : (b + 1) * BLOCK, pl.ds(first, HALF)].T
        r = lax.broadcasted_iota(jnp.int32, (HALF, BLOCK), 0) + first
        c = lax.broadcasted_iota(jnp.int32, (HALF, BLOCK), 1) + b * BLOCK
        factor_out[:, b * BLOCK : (b + 1) * BLOCK] = jnp.where(r >= c, block, 0.0)


def factor_and_inverse(mine, other, core):
    return pl.pallas_call(
        factor_kernel,
        out_shape=(
            jax.ShapeDtypeStruct((HALF, TILE), F32),
            jax.ShapeDtypeStruct((TILE, TILE), F32),
        ),
        in_specs=[pl.BlockSpec(memory_space=pltpu.SMEM)]
        + [pl.BlockSpec(memory_space=pltpu.VMEM)] * 2,
        out_specs=[pl.BlockSpec(memory_space=pltpu.VMEM)] * 2,
        scratch_shapes=[pltpu.VMEM((TILE, TILE), F32)] * 2 + [pltpu.VMEM((NB, 2 * NB), F32)] * 2
        + [pltpu.VMEM((TILE, NB), F32)],
        compiler_params=params(),
        cost_estimate=pl.CostEstimate(
            flops=10**9, bytes_accessed=5 * 2**20, transcendentals=0
        ),
    )(core.reshape(1), mine, other)


def local(panel_tiles, left_u, earlier_right_factors, tile_global_index):
    tile_count = tile_global_index.shape[0]
    pivot_position = jnp.sum(
        jnp.where(tile_global_index == 0, jnp.arange(tile_count, dtype=jnp.int32), 0)
    )
    owner = pivot_position >> 1
    slot = pivot_position & 1
    away = {
        "x": (lax.axis_index("x") - owner) & 3,
        "y": (lax.axis_index("y") - (owner >> 2)) & 3,
        "zl": (lax.axis_index("zl") - (owner >> 4)) & 1,
    }
    zh, core = lax.axis_index("zh"), lax.axis_index("core")
    my_col = lax.axis_index(COL)

    def slot_quarters(value):
        return [
            lax.dynamic_slice_in_dim(value, slot * TILE + k * BLOCK, BLOCK, 0) for k in range(4)
        ]

    where = {a: jnp.stack([(away[a] - k) & 3 for k in range(4)]) for a in ("x", "y")}
    quad = jnp.stack([2 * zh + core, 2 * zh + 1 - core, 2 - 2 * zh + core, 3 - 2 * zh - core])
    square = jnp.arange(16, dtype=jnp.int32)
    sixteen = jnp.concatenate([(square - owner) & 3, ((square >> 2) - (owner >> 2)) & 3, quad[::-1]])
    holds = away["zl"] == 0

    def slot_quarters(value):
        return [
            lax.dynamic_slice_in_dim(value, slot * TILE + k * BLOCK, BLOCK, 0) for k in range(4)
        ]

    tiles = [lax.dynamic_slice_in_dim(panel_tiles, z * TILE, TILE, 0) for z in (zh, 1 - zh)]
    tiles = [tiles[0], shift(tiles[1], "zh", 1)]

    v, u = slot_quarters(earlier_right_factors), slot_quarters(left_u)
    *u, slot = in_step(*u, slot)
    v1, v3 = neighbours(v, "x")
    u1, u3 = neighbours(u, "y")
    upper = pivot_update(left_u, earlier_right_factors, panel_tiles, slot, my_col, core)
    s = upper[0] + shift(upper[1], "core", 1)
    v2, u2, v1, v3, u1, u3, _, tiles[1] = in_step(v[2], u[2], v1, v3, u1, u3, s, tiles[1])
    s = (s + shift(s, "zh", 1)).reshape(5 * BLOCK, BLOCK)
    own = [lax.dynamic_slice_in_dim(t, core * HALF, HALF, 0) for t in tiles]
    sent = [lax.dynamic_slice_in_dim(t, (1 - core) * HALF, HALF, 0) for t in tiles]
    sent = [shift(t, "core", 1) for t in sent]
    panel_rows = place([own[0], sent[0], own[1], sent[1]], quad, 1)
    v = lax.select_n(away["x"], v[0], v1, shift(v2, "x", 2), v3)
    u = lax.select_n(away["y"], u[0], u1, shift(u2, "y", 2), u3)
    v, u, panel_rows = in_step(v, u, panel_rows)
    v, u = sends(quarters(v), "y"), sends(quarters(u), "x")
    v, u, s = in_step(lax.select_n(away["y"], *v), lax.select_n(away["x"], *u), s)
    v = jnp.where(holds, v, shift(v, "zl", 1))
    u = jnp.where(holds, u, shift(u, "zl", 1))
    gathered = lax.all_gather(jnp.concatenate([v, u], axis=1), ("y", "x"))

    s = lax.select_n(away["x"], *sends(quarters(s), "x"))
    s = lax.select_n(away["y"], *sends(quarters(s), "y"))
    s = jnp.where(holds, s, shift(s, "zl", 1))
    s = place(pieces(s, "y"), where["y"])
    mine = place(pieces(s, "x"), where["x"]).reshape(5, BLOCK, BLOCK)
    other = shift(mine, "core", 1)

    gathered, mine, other, panel_rows = in_step(gathered, mine, other, panel_rows)
    far_other, far, near_other, near = update(left_u, earlier_right_factors, gathered, sixteen)
    far = far + shift(far_other, "core", 1)
    near = near + shift(near_other, "core", 1)
    far, near, mine, other = in_step(far, panel_rows - near, mine, other)
    far = shift(far, "zh", 1)
    factor_rows, inverse = factor_and_inverse(mine, other, core)
    updated = near - far

    chosen = jnp.logical_and(lax.axis_index(ROW) == owner, slot == zh)

    def solved(z):
        inv = lax.dynamic_slice_in_dim(inverse, z * HALF, HALF, 0)
        fac = lax.dynamic_slice_in_dim(factor_rows, z * HALF, HALF, 1)
        return jnp.where(chosen, fac, dot(updated, inv, 1, 1, lax.Precision.HIGH))

    def column(value, c):
        return lax.dynamic_slice_in_dim(value, c * BLOCK, BLOCK, 1)

    out_far = shift(solved(1 - zh), "zh", 1)
    out_near = solved(zh)
    out = [column(out_near, core), shift(column(out_near, 1 - core), "core", 1)]
    out += [column(out_far, core), shift(column(out_far, 1 - core), "core", 1)]
    return place(out, quad)


def solution(mesh):
    split = Mesh(mesh.devices.reshape(2, 4, 4, 2, 2), ("zl", "y", "x", "zh", "core"))
    return jax.shard_map(
        local,
        mesh=split,
        in_specs=(P(ROW, COL), P(ROW, COL), P(ROW, COL), P()),
        out_specs=P(ROW, COL),
        check_vma=False,
    )
```

```python
import functools

import jax
import jax.numpy as jnp
from jax import lax
from jax.experimental import pallas as pl
from jax.experimental.pallas import tpu as pltpu
from jax.sharding import Mesh
from jax.sharding import PartitionSpec as P

TILE = 1024
RANK = 256
TILE_DEV = 2
COL_DEV = 6
BLOCK = 256
HALF = 512
ROW = ("zl", "y", "x")
COL = ("zh", "core")
UPPER = ((0, 0), (1, 1), (2, 2), (0, 1), (0, 2), (3, 3), (1, 2), (2, 3), (1, 3), (0, 3))
NB = 128
STRIP = 32
F32 = jnp.float32
HIGHEST = lax.Precision.HIGHEST


def shift(value, axis, step):
    devices = lax.axis_size(axis)
    return lax.ppermute(value, axis, [(i, (i + step) % devices) for i in range(devices)])


def dot(a, b, ca, cb, precision=None):
    return lax.dot_general(
        a, b, (((ca,), (cb,)), ((), ())), precision=precision, preferred_element_type=F32
    )


def params():
    return pltpu.CompilerParams(vmem_limit_bytes=48 << 20)


def place_kernel(axis, where_ref, *refs):
    out = refs[-1]
    for k, ref in enumerate(refs[:-1]):
        size = ref.shape[axis]
        part = pl.ds(pl.multiple_of(where_ref[k] * size, size), size)
        if axis == 0:
            out[part, :] = ref[...]
        else:
            out[:, part] = ref[...]


def place(values, where, axis=0):
    shape = list(values[0].shape)
    shape[axis] *= len(values)
    size = shape[0] * shape[1] * values[0].dtype.itemsize
    return pl.pallas_call(
        functools.partial(place_kernel, axis),
        out_shape=jax.ShapeDtypeStruct(shape, values[0].dtype),
        in_specs=[pl.BlockSpec(memory_space=pltpu.SMEM)]
        + [pl.BlockSpec(memory_space=pltpu.VMEM)] * len(values),
        out_specs=pl.BlockSpec(memory_space=pltpu.VMEM),
        compiler_params=params(),
        cost_estimate=pl.CostEstimate(flops=0, bytes_accessed=2 * size, transcendentals=0),
    )(where, *values)


def in_step(*values):
    return lax.optimization_barrier(values)


def quarters(value):
    rows = value.shape[0] // 4
    return [value[k * rows : (k + 1) * rows] for k in range(4)]


def sends(parts, axis):
    return [parts[0]] + [shift(parts[k], axis, k) for k in (1, 2, 3)]


def neighbours(parts, axis):
    return shift(parts[1], axis, 1), shift(parts[3], axis, 3)


def pieces(piece, axis):
    return sends([piece] * 4, axis)


def update_kernel(where_ref, left, right, right_pieces, left_pieces, *refs):
    outs, (pivot_right, pivot_left, total) = refs[:4], refs[4:]
    j = pl.program_id(0)

    @pl.when(j == 0)
    def _():
        total[...] = jnp.zeros_like(total)

    size = left_pieces.shape[1]
    for k in range(left_pieces.shape[0]):
        x, y = where_ref[k], where_ref[16 + k]
        pivot_right[pl.ds(pl.multiple_of((4 * x + y) * size, size), size), :] = right_pieces[k]
        pivot_left[pl.ds(pl.multiple_of((4 * y + x) * size, size), size), :] = left_pieces[k]
    turned = pivot_right[...].T
    for t in range(TILE_DEV):
        rows = slice(t * TILE, (t + 1) * TILE)
        inner = dot(turned, right[rows, :], 1, 0).astype(jnp.bfloat16)
        product = dot(left[rows, :], inner, 1, 1).astype(jnp.bfloat16)
        for h in range(2):
            total[2 * t + h] += dot(product[h * HALF : (h + 1) * HALF], pivot_left[...], 1, 1)

    @pl.when(j == COL_DEV - 1)
    def _():
        for k, out in enumerate(outs):
            out[...] = total[where_ref[32 + k]]


def update(left, right, gathered, where):
    rows, columns = left.shape
    count, size = gathered.shape[:2]
    steps = columns // RANK
    both = pl.BlockSpec((rows, RANK), lambda j, s: (0, j))
    return pl.pallas_call(
        update_kernel,
        out_shape=[jax.ShapeDtypeStruct((HALF, TILE), F32)] * 4,
        grid_spec=pltpu.PrefetchScalarGridSpec(
            num_scalar_prefetch=1,
            grid=(steps,),
            in_specs=[
                both,
                both,
                pl.BlockSpec((count, size, RANK), lambda j, s: (0, 0, j)),
                pl.BlockSpec((count, size, RANK), lambda j, s: (0, 0, j + steps)),
            ],
            out_specs=[pl.BlockSpec((HALF, TILE), lambda j, s: (0, 0))] * 4,
            scratch_shapes=[pltpu.VMEM((TILE, RANK), jnp.bfloat16)] * 2
            + [pltpu.VMEM((4, HALF, TILE), F32)],
        ),
        compiler_params=params(),
        cost_estimate=pl.CostEstimate(
            flops=12 * rows * columns * RANK, bytes_accessed=8 * rows * columns, transcendentals=0
        ),
    )(where, left, right, gathered, gathered)


def pivot_kernel(where_ref, left, right, panel, out, total):
    j = pl.program_id(0)

    @pl.when(j == 0)
    def _():
        total[...] = jnp.zeros_like(total)
        start = pl.multiple_of(where_ref[1] * BLOCK, BLOCK)
        total[:, pl.ds(start, BLOCK)] = panel[...]

    inner = dot(right[...], right[...], 0, 0).astype(jnp.bfloat16)
    product = dot(left[...], inner, 1, 0).astype(jnp.bfloat16)
    total[...] -= dot(product, left[...], 1, 1)

    @pl.when(j == COL_DEV - 1)
    def _():
        core = where_ref[2]
        for b, (r, c) in enumerate(UPPER):
            above = total[r * BLOCK : (r + 1) * BLOCK, c * BLOCK : (c + 1) * BLOCK]
            below = total[c * BLOCK : (c + 1) * BLOCK, r * BLOCK : (r + 1) * BLOCK]
            out[jnp.where(core == b // 5, 0, 1), b % 5] = (above + below.T) * 0.5


def pivot_update(left, right, panel, slot, my_col, core):
    tile = pl.BlockSpec((TILE, RANK), lambda j, s: (s[0], j))
    return pl.pallas_call(
        pivot_kernel,
        out_shape=jax.ShapeDtypeStruct((2, 5, BLOCK, BLOCK), F32),
        grid_spec=pltpu.PrefetchScalarGridSpec(
            num_scalar_prefetch=1,
            grid=(COL_DEV,),
            in_specs=[tile, tile, pl.BlockSpec((TILE, BLOCK), lambda j, s: (s[0], 0))],
            out_specs=pl.BlockSpec((2, 5, BLOCK, BLOCK), lambda j, s: (0, 0, 0, 0)),
            scratch_shapes=[pltpu.VMEM((TILE, TILE), F32)],
        ),
        compiler_params=params(),
        cost_estimate=pl.CostEstimate(
            flops=10**6, bytes_accessed=10**4, transcendentals=0
        ),
    )(jnp.stack([slot, my_col, core]), left, right, panel)


def factor_kernel(where_ref, mine, other, factor_out, inverse_out, u_ref, x_ref, m_ref, f_ref, w_ref):
    for b, (r, c) in enumerate(UPPER):
        block = jnp.where(where_ref[0] == b // 5, mine[b % 5], other[b % 5])
        u_ref[r * BLOCK : (r + 1) * BLOCK, c * BLOCK : (c + 1) * BLOCK] = block
    x_ref[...] = jnp.zeros_like(x_ref)
    row = lax.broadcasted_iota(jnp.int32, (NB, NB), 0)
    column = lax.broadcasted_iota(jnp.int32, (NB, NB), 1)
    strip_row = lax.broadcasted_iota(jnp.int32, (STRIP, NB), 0)
    for k in range(TILE // NB):
        k0, k1 = k * NB, (k + 1) * NB
        m_ref[:, :NB] = u_ref[k0:k1, k0:k1]
        m_ref[:, NB:] = jnp.where(row == column, 1.0, 0.0).astype(F32)

        def strip(t, carry):
            start = pl.multiple_of(t * STRIP, STRIP)
            if k and k1 < TILE:
                size = (TILE - k1) // (NB // STRIP)
                wt = w_ref[pl.ds(pl.multiple_of(t * size, size), size), :]
                rows = pl.ds(pl.multiple_of(k1 + t * size, STRIP), size)
                u_ref[rows, k1:] -= dot(wt, u_ref[k0 - NB : k0, k1:], 1, 0, HIGHEST)
                x_ref[rows, :k0] -= dot(wt, x_ref[k0 - NB : k0, :k0], 1, 0, HIGHEST)
            ps = m_ref[pl.ds(start, STRIP), :NB]
            pi = m_ref[pl.ds(start, STRIP), NB:]
            turned = pltpu.roll(ps, NB - start, 1)
            c = [jnp.broadcast_to(turned[:, j : j + 1], (STRIP, NB)) for j in range(STRIP)]
            for j in range(STRIP):
                inv = lax.rsqrt(jnp.broadcast_to(c[j][j : j + 1, :], (STRIP, NB)))
                col = c[j] * inv
                for q in range(j + 1, STRIP):
                    c[q] = c[q] - col * jnp.broadcast_to(col[q : q + 1, :], (STRIP, NB))
                us = jnp.broadcast_to(ps[j : j + 1, :], (STRIP, NB)) * inv
                ui = jnp.broadcast_to(pi[j : j + 1, :], (STRIP, NB)) * inv
                below = jnp.where(strip_row > j, col, 0.0)
                ps = jnp.where(strip_row == j, us, ps - below * us)
                pi = jnp.where(strip_row == j, ui, pi - below * ui)
            f_ref[pl.ds(start, STRIP), :NB] = ps
            f_ref[pl.ds(start, STRIP), NB:] = pi

            @pl.when(t < NB // STRIP - 1)
            def _():
                m_ref[:, :NB] -= dot(ps, ps, 0, 0, HIGHEST)
                m_ref[:, NB:] -= dot(ps, pi, 0, 0, HIGHEST)

            return carry

        lax.fori_loop(0, NB // STRIP, strip, 0)
        xk = f_ref[:, NB:]
        u_ref[k0:k1, k0:k1] = f_ref[:, :NB]
        if k:
            x_ref[k0:k1, :k0] = dot(xk, x_ref[k0:k1, :k0], 1, 0, HIGHEST)
        x_ref[k0:k1, k0:k1] = xk
        if k1 < TILE:
            w = dot(xk, u_ref[k0:k1, k1:], 1, 0, HIGHEST)
            u_ref[k0:k1, k1:] = w
            k2 = k1 + NB
            u_ref[k1:k2, k1:] -= dot(w[:, :NB], w, 0, 0, HIGHEST)
            x_ref[k1:k2, :k1] -= dot(w[:, :NB], x_ref[k0:k1, :k1], 0, 0, HIGHEST)
            if k2 < TILE:
                w_ref[: TILE - k2, :] = w[:, NB:].T
    inverse_out[...] = x_ref[...]
    first = pl.multiple_of(where_ref[0] * HALF, HALF)
    for b in range(4):
        block = u_ref[b * BLOCK : (b + 1) * BLOCK, pl.ds(first, HALF)].T
        r = lax.broadcasted_iota(jnp.int32, (HALF, BLOCK), 0) + first
        c = lax.broadcasted_iota(jnp.int32, (HALF, BLOCK), 1) + b * BLOCK
        factor_out[:, b * BLOCK : (b + 1) * BLOCK] = jnp.where(r >= c, block, 0.0)


def factor_and_inverse(mine, other, core):
    return pl.pallas_call(
        factor_kernel,
        out_shape=(
            jax.ShapeDtypeStruct((HALF, TILE), F32),
            jax.ShapeDtypeStruct((TILE, TILE), F32),
        ),
        in_specs=[pl.BlockSpec(memory_space=pltpu.SMEM)]
        + [pl.BlockSpec(memory_space=pltpu.VMEM)] * 2,
        out_specs=[pl.BlockSpec(memory_space=pltpu.VMEM)] * 2,
        scratch_shapes=[pltpu.VMEM((TILE, TILE), F32)] * 2 + [pltpu.VMEM((NB, 2 * NB), F32)] * 2
        + [pltpu.VMEM((TILE, NB), F32)],
        compiler_params=params(),
        cost_estimate=pl.CostEstimate(
            flops=10**9, bytes_accessed=5 * 2**20, transcendentals=0
        ),
    )(core.reshape(1), mine, other)


def local(panel_tiles, left_u, earlier_right_factors, tile_global_index):
    tile_count = tile_global_index.shape[0]
    pivot_position = jnp.sum(
        jnp.where(tile_global_index == 0, jnp.arange(tile_count, dtype=jnp.int32), 0)
    )
    owner = pivot_position >> 1
    slot = pivot_position & 1
    away = {
        "x": (lax.axis_index("x") - owner) & 3,
        "y": (lax.axis_index("y") - (owner >> 2)) & 3,
        "zl": (lax.axis_index("zl") - (owner >> 4)) & 1,
    }
    zh, core = lax.axis_index("zh"), lax.axis_index("core")
    my_col = lax.axis_index(COL)

    def slot_quarters(value):
        return [
            lax.dynamic_slice_in_dim(value, slot * TILE + k * BLOCK, BLOCK, 0) for k in range(4)
        ]

    where = {a: jnp.stack([(away[a] - k) & 3 for k in range(4)]) for a in ("x", "y")}
    quad = jnp.stack([2 * zh + core, 2 * zh + 1 - core, 2 - 2 * zh + core, 3 - 2 * zh - core])
    square = jnp.arange(16, dtype=jnp.int32)
    sixteen = jnp.concatenate([(square - owner) & 3, ((square >> 2) - (owner >> 2)) & 3, quad[::-1]])
    holds = away["zl"] == 0

    def slot_quarters(value):
        return [
            lax.dynamic_slice_in_dim(value, slot * TILE + k * BLOCK, BLOCK, 0) for k in range(4)
        ]

    tiles = [lax.dynamic_slice_in_dim(panel_tiles, z * TILE, TILE, 0) for z in (zh, 1 - zh)]
    tiles = [tiles[0], shift(tiles[1], "zh", 1)]

    v, u = slot_quarters(earlier_right_factors), slot_quarters(left_u)
    *u, slot = in_step(*u, slot)
    v1, v3 = neighbours(v, "x")
    u1, u3 = neighbours(u, "y")
    upper = pivot_update(left_u, earlier_right_factors, panel_tiles, slot, my_col, core)
    s = upper[0] + shift(upper[1], "core", 1)
    v2, u2, v1, v3, u1, u3, _, tiles[1] = in_step(v[2], u[2], v1, v3, u1, u3, s, tiles[1])
    s = (s + shift(s, "zh", 1)).reshape(5 * BLOCK, BLOCK)
    own = [lax.dynamic_slice_in_dim(t, core * HALF, HALF, 0) for t in tiles]
    sent = [lax.dynamic_slice_in_dim(t, (1 - core) * HALF, HALF, 0) for t in tiles]
    sent = [shift(t, "core", 1) for t in sent]
    panel_rows = place([own[0], sent[0], own[1], sent[1]], quad, 1)
    v = lax.select_n(away["x"], v[0], v1, shift(v2, "x", 2), v3)
    u = lax.select_n(away["y"], u[0], u1, shift(u2, "y", 2), u3)
    v, u, panel_rows = in_step(v, u, panel_rows)
    v, u = sends(quarters(v), "y"), sends(quarters(u), "x")
    v, u, s = in_step(lax.select_n(away["y"], *v), lax.select_n(away["x"], *u), s)
    v = jnp.where(holds, v, shift(v, "zl", 1))
    u = jnp.where(holds, u, shift(u, "zl", 1))
    gathered = lax.all_gather(jnp.concatenate([v, u], axis=1), ("y", "x"))

    s = lax.select_n(away["x"], *sends(quarters(s), "x"))
    s = lax.select_n(away["y"], *sends(quarters(s), "y"))
    s = jnp.where(holds, s, shift(s, "zl", 1))
    s = place(pieces(s, "y"), where["y"])
    mine = place(pieces(s, "x"), where["x"]).reshape(5, BLOCK, BLOCK)
    other = shift(mine, "core", 1)

    gathered, mine, other, panel_rows = in_step(gathered, mine, other, panel_rows)
    far_other, far, near_other, near = update(left_u, earlier_right_factors, gathered, sixteen)
    far = far + shift(far_other, "core", 1)
    near = near + shift(near_other, "core", 1)
    far, near, mine, other = in_step(far, panel_rows - near, mine, other)
    far = shift(far, "zh", 1)
    factor_rows, inverse = factor_and_inverse(mine, other, core)
    updated = near - far

    chosen = jnp.logical_and(lax.axis_index(ROW) == owner, slot == zh)

    def solved(z):
        inv = lax.dynamic_slice_in_dim(inverse, z * HALF, HALF, 0)
        fac = lax.dynamic_slice_in_dim(factor_rows, z * HALF, HALF, 1)
        return jnp.where(chosen, fac, dot(updated, inv, 1, 1, lax.Precision.HIGH))

    def column(value, c):
        return lax.dynamic_slice_in_dim(value, c * BLOCK, BLOCK, 1)

    out_far = solved(1 - zh)
    scale = jnp.maximum(jnp.max(jnp.abs(out_far), axis=1), 1e-30)
    sent = shift((out_far / scale[:, None]).astype(jnp.float16), "zh", 1)
    out_far = sent.astype(F32) * shift(scale, "zh", 1)[:, None]
    out_near = solved(zh)
    out = [column(out_near, core), shift(column(out_near, 1 - core), "core", 1)]
    out += [column(out_far, core), shift(column(out_far, 1 - core), "core", 1)]
    return place(out, quad)


def solution(mesh):
    split = Mesh(mesh.devices.reshape(2, 4, 4, 2, 2), ("zl", "y", "x", "zh", "core"))
    return jax.shard_map(
        local,
        mesh=split,
        in_specs=(P(ROW, COL), P(ROW, COL), P(ROW, COL), P()),
        out_specs=P(ROW, COL),
        check_vma=False,
    )
```

```python
import functools

import jax
import jax.numpy as jnp
from jax import lax
from jax.experimental import pallas as pl
from jax.experimental.pallas import tpu as pltpu
from jax.sharding import Mesh
from jax.sharding import PartitionSpec as P

TILE = 1024
RANK = 256
TILE_DEV = 2
COL_DEV = 6
BLOCK = 256
HALF = 512
ROW = ("zl", "y", "x")
COL = ("zh", "core")
UPPER = ((0, 0), (1, 1), (2, 2), (0, 1), (0, 2), (3, 3), (1, 2), (2, 3), (1, 3), (0, 3))
NB = 128
STRIP = 32
F32 = jnp.float32
HIGHEST = lax.Precision.HIGHEST


def shift(value, axis, step):
    devices = lax.axis_size(axis)
    return lax.ppermute(value, axis, [(i, (i + step) % devices) for i in range(devices)])


def dot(a, b, ca, cb, precision=None):
    return lax.dot_general(
        a, b, (((ca,), (cb,)), ((), ())), precision=precision, preferred_element_type=F32
    )


def params():
    return pltpu.CompilerParams(vmem_limit_bytes=48 << 20)


def place_kernel(axis, where_ref, *refs):
    out = refs[-1]
    for k, ref in enumerate(refs[:-1]):
        size = ref.shape[axis]
        part = pl.ds(pl.multiple_of(where_ref[k] * size, size), size)
        if axis == 0:
            out[part, :] = ref[...]
        else:
            out[:, part] = ref[...]


def place(values, where, axis=0):
    shape = list(values[0].shape)
    shape[axis] *= len(values)
    size = shape[0] * shape[1] * values[0].dtype.itemsize
    return pl.pallas_call(
        functools.partial(place_kernel, axis),
        out_shape=jax.ShapeDtypeStruct(shape, values[0].dtype),
        in_specs=[pl.BlockSpec(memory_space=pltpu.SMEM)]
        + [pl.BlockSpec(memory_space=pltpu.VMEM)] * len(values),
        out_specs=pl.BlockSpec(memory_space=pltpu.VMEM),
        compiler_params=params(),
        cost_estimate=pl.CostEstimate(flops=0, bytes_accessed=2 * size, transcendentals=0),
    )(where, *values)


def in_step(*values):
    return lax.optimization_barrier(values)


def quarters(value):
    rows = value.shape[0] // 4
    return [value[k * rows : (k + 1) * rows] for k in range(4)]


def sends(parts, axis):
    return [parts[0]] + [shift(parts[k], axis, k) for k in (1, 2, 3)]


def neighbours(parts, axis):
    return shift(parts[1], axis, 1), shift(parts[3], axis, 3)


def pieces(piece, axis):
    return sends([piece] * 4, axis)


def update_kernel(where_ref, left, right, right_pieces, left_pieces, *refs):
    outs, (pivot_right, pivot_left, total) = refs[:4], refs[4:]
    j = pl.program_id(0)

    @pl.when(j == 0)
    def _():
        total[...] = jnp.zeros_like(total)

    size = left_pieces.shape[1]
    for k in range(left_pieces.shape[0]):
        x, y = where_ref[k], where_ref[16 + k]
        pivot_right[pl.ds(pl.multiple_of((4 * x + y) * size, size), size), :] = right_pieces[k]
        pivot_left[pl.ds(pl.multiple_of((4 * y + x) * size, size), size), :] = left_pieces[k]
    turned = pivot_right[...].T
    for t in range(TILE_DEV):
        rows = slice(t * TILE, (t + 1) * TILE)
        inner = dot(turned, right[rows, :], 1, 0).astype(jnp.bfloat16)
        product = dot(left[rows, :], inner, 1, 1).astype(jnp.bfloat16)
        for h in range(2):
            total[2 * t + h] += dot(product[h * HALF : (h + 1) * HALF], pivot_left[...], 1, 1)

    @pl.when(j == COL_DEV - 1)
    def _():
        for k, out in enumerate(outs):
            out[...] = total[where_ref[32 + k]]


def update(left, right, gathered, where):
    rows, columns = left.shape
    count, size = gathered.shape[:2]
    steps = columns // RANK
    both = pl.BlockSpec((rows, RANK), lambda j, s: (0, j))
    return pl.pallas_call(
        update_kernel,
        out_shape=[jax.ShapeDtypeStruct((HALF, TILE), F32)] * 4,
        grid_spec=pltpu.PrefetchScalarGridSpec(
            num_scalar_prefetch=1,
            grid=(steps,),
            in_specs=[
                both,
                both,
                pl.BlockSpec((count, size, RANK), lambda j, s: (0, 0, j)),
                pl.BlockSpec((count, size, RANK), lambda j, s: (0, 0, j + steps)),
            ],
            out_specs=[pl.BlockSpec((HALF, TILE), lambda j, s: (0, 0))] * 4,
            scratch_shapes=[pltpu.VMEM((TILE, RANK), jnp.bfloat16)] * 2
            + [pltpu.VMEM((4, HALF, TILE), F32)],
        ),
        compiler_params=params(),
        cost_estimate=pl.CostEstimate(
            flops=12 * rows * columns * RANK, bytes_accessed=8 * rows * columns, transcendentals=0
        ),
    )(where, left, right, gathered, gathered)


def pivot_kernel(where_ref, left, right, panel, out, total):
    j = pl.program_id(0)

    @pl.when(j == 0)
    def _():
        total[...] = jnp.zeros_like(total)
        start = pl.multiple_of(where_ref[1] * BLOCK, BLOCK)
        total[:, pl.ds(start, BLOCK)] = panel[...]

    inner = dot(right[...], right[...], 0, 0).astype(jnp.bfloat16)
    product = dot(left[...], inner, 1, 0).astype(jnp.bfloat16)
    total[...] -= dot(product, left[...], 1, 1)

    @pl.when(j == COL_DEV - 1)
    def _():
        core = where_ref[2]
        for b, (r, c) in enumerate(UPPER):
            above = total[r * BLOCK : (r + 1) * BLOCK, c * BLOCK : (c + 1) * BLOCK]
            below = total[c * BLOCK : (c + 1) * BLOCK, r * BLOCK : (r + 1) * BLOCK]
            out[jnp.where(core == b // 5, 0, 1), b % 5] = (above + below.T) * 0.5


def pivot_update(left, right, panel, slot, my_col, core):
    tile = pl.BlockSpec((TILE, RANK), lambda j, s: (s[0], j))
    return pl.pallas_call(
        pivot_kernel,
        out_shape=jax.ShapeDtypeStruct((2, 5, BLOCK, BLOCK), F32),
        grid_spec=pltpu.PrefetchScalarGridSpec(
            num_scalar_prefetch=1,
            grid=(COL_DEV,),
            in_specs=[tile, tile, pl.BlockSpec((TILE, BLOCK), lambda j, s: (s[0], 0))],
            out_specs=pl.BlockSpec((2, 5, BLOCK, BLOCK), lambda j, s: (0, 0, 0, 0)),
            scratch_shapes=[pltpu.VMEM((TILE, TILE), F32)],
        ),
        compiler_params=params(),
        cost_estimate=pl.CostEstimate(
            flops=10**6, bytes_accessed=10**4, transcendentals=0
        ),
    )(jnp.stack([slot, my_col, core]), left, right, panel)


def factor_kernel(where_ref, mine, other, factor_out, inverse_out, u_ref, x_ref, m_ref, f_ref, w_ref):
    for b, (r, c) in enumerate(UPPER):
        block = jnp.where(where_ref[0] == b // 5, mine[b % 5], other[b % 5])
        u_ref[r * BLOCK : (r + 1) * BLOCK, c * BLOCK : (c + 1) * BLOCK] = block
    x_ref[...] = jnp.zeros_like(x_ref)
    row = lax.broadcasted_iota(jnp.int32, (NB, NB), 0)
    column = lax.broadcasted_iota(jnp.int32, (NB, NB), 1)
    strip_row = lax.broadcasted_iota(jnp.int32, (STRIP, NB), 0)
    for k in range(TILE // NB):
        k0, k1 = k * NB, (k + 1) * NB
        m_ref[:, :NB] = u_ref[k0:k1, k0:k1]
        m_ref[:, NB:] = jnp.where(row == column, 1.0, 0.0).astype(F32)

        def strip(t, carry):
            start = pl.multiple_of(t * STRIP, STRIP)
            if k and k1 < TILE:
                size = (TILE - k1) // (NB // STRIP)
                wt = w_ref[pl.ds(pl.multiple_of(t * size, size), size), :]
                rows = pl.ds(pl.multiple_of(k1 + t * size, STRIP), size)
                u_ref[rows, k1:] -= dot(wt, u_ref[k0 - NB : k0, k1:], 1, 0, HIGHEST)
                x_ref[rows, :k0] -= dot(wt, x_ref[k0 - NB : k0, :k0], 1, 0, HIGHEST)
            ps = m_ref[pl.ds(start, STRIP), :NB]
            pi = m_ref[pl.ds(start, STRIP), NB:]
            turned = pltpu.roll(ps, NB - start, 1)
            c = [jnp.broadcast_to(turned[:, j : j + 1], (STRIP, NB)) for j in range(STRIP)]
            for j in range(STRIP):
                inv = lax.rsqrt(jnp.broadcast_to(c[j][j : j + 1, :], (STRIP, NB)))
                col = c[j] * inv
                for q in range(j + 1, STRIP):
                    c[q] = c[q] - col * jnp.broadcast_to(col[q : q + 1, :], (STRIP, NB))
                us = jnp.broadcast_to(ps[j : j + 1, :], (STRIP, NB)) * inv
                ui = jnp.broadcast_to(pi[j : j + 1, :], (STRIP, NB)) * inv
                below = jnp.where(strip_row > j, col, 0.0)
                ps = jnp.where(strip_row == j, us, ps - below * us)
                pi = jnp.where(strip_row == j, ui, pi - below * ui)
            f_ref[pl.ds(start, STRIP), :NB] = ps
            f_ref[pl.ds(start, STRIP), NB:] = pi

            @pl.when(t < NB // STRIP - 1)
            def _():
                m_ref[:, :NB] -= dot(ps, ps, 0, 0, HIGHEST)
                m_ref[:, NB:] -= dot(ps, pi, 0, 0, HIGHEST)

            return carry

        lax.fori_loop(0, NB // STRIP, strip, 0)
        xk = f_ref[:, NB:]
        u_ref[k0:k1, k0:k1] = f_ref[:, :NB]
        if k:
            x_ref[k0:k1, :k0] = dot(xk, x_ref[k0:k1, :k0], 1, 0, HIGHEST)
        x_ref[k0:k1, k0:k1] = xk
        if k1 < TILE:
            w = dot(xk, u_ref[k0:k1, k1:], 1, 0, HIGHEST)
            u_ref[k0:k1, k1:] = w
            k2 = k1 + NB
            u_ref[k1:k2, k1:] -= dot(w[:, :NB], w, 0, 0, HIGHEST)
            x_ref[k1:k2, :k1] -= dot(w[:, :NB], x_ref[k0:k1, :k1], 0, 0, HIGHEST)
            if k2 < TILE:
                w_ref[: TILE - k2, :] = w[:, NB:].T
    inverse_out[...] = x_ref[...]
    first = pl.multiple_of(where_ref[0] * HALF, HALF)
    for b in range(4):
        block = u_ref[b * BLOCK : (b + 1) * BLOCK, pl.ds(first, HALF)].T
        r = lax.broadcasted_iota(jnp.int32, (HALF, BLOCK), 0) + first
        c = lax.broadcasted_iota(jnp.int32, (HALF, BLOCK), 1) + b * BLOCK
        factor_out[:, b * BLOCK : (b + 1) * BLOCK] = jnp.where(r >= c, block, 0.0)


def factor_and_inverse(mine, other, core):
    return pl.pallas_call(
        factor_kernel,
        out_shape=(
            jax.ShapeDtypeStruct((HALF, TILE), F32),
            jax.ShapeDtypeStruct((TILE, TILE), F32),
        ),
        in_specs=[pl.BlockSpec(memory_space=pltpu.SMEM)]
        + [pl.BlockSpec(memory_space=pltpu.VMEM)] * 2,
        out_specs=[pl.BlockSpec(memory_space=pltpu.VMEM)] * 2,
        scratch_shapes=[pltpu.VMEM((TILE, TILE), F32)] * 2 + [pltpu.VMEM((NB, 2 * NB), F32)] * 2
        + [pltpu.VMEM((TILE, NB), F32)],
        compiler_params=params(),
        cost_estimate=pl.CostEstimate(
            flops=10**9, bytes_accessed=5 * 2**20, transcendentals=0
        ),
    )(core.reshape(1), mine, other)


def local(panel_tiles, left_u, earlier_right_factors, tile_global_index):
    tile_count = tile_global_index.shape[0]
    pivot_position = jnp.sum(
        jnp.where(tile_global_index == 0, jnp.arange(tile_count, dtype=jnp.int32), 0)
    )
    owner = pivot_position >> 1
    slot = pivot_position & 1
    away = {
        "x": (lax.axis_index("x") - owner) & 3,
        "y": (lax.axis_index("y") - (owner >> 2)) & 3,
        "zl": (lax.axis_index("zl") - (owner >> 4)) & 1,
    }
    zh, core = lax.axis_index("zh"), lax.axis_index("core")
    my_col = lax.axis_index(COL)

    def slot_quarters(value):
        return [
            lax.dynamic_slice_in_dim(value, slot * TILE + k * BLOCK, BLOCK, 0) for k in range(4)
        ]

    where = {a: jnp.stack([(away[a] - k) & 3 for k in range(4)]) for a in ("x", "y")}
    quad = jnp.stack([2 * zh + core, 2 * zh + 1 - core, 2 - 2 * zh + core, 3 - 2 * zh - core])
    square = jnp.arange(16, dtype=jnp.int32)
    sixteen = jnp.concatenate([(square - owner) & 3, ((square >> 2) - (owner >> 2)) & 3, quad[::-1]])
    holds = away["zl"] == 0

    def slot_quarters(value):
        return [
            lax.dynamic_slice_in_dim(value, slot * TILE + k * BLOCK, BLOCK, 0) for k in range(4)
        ]

    tiles = [lax.dynamic_slice_in_dim(panel_tiles, z * TILE, TILE, 0) for z in (zh, 1 - zh)]
    tiles = [tiles[0], shift(tiles[1], "zh", 1)]

    v, u = slot_quarters(earlier_right_factors), slot_quarters(left_u)
    *u, slot = in_step(*u, slot)
    v1, v3 = neighbours(v, "x")
    u1, u3 = neighbours(u, "y")
    upper = pivot_update(left_u, earlier_right_factors, panel_tiles, slot, my_col, core)
    s = upper[0] + shift(upper[1], "core", 1)
    v2, u2, v1, v3, u1, u3, _ = in_step(v[2], u[2], v1, v3, u1, u3, s)
    s = (s + shift(s, "zh", 1)).reshape(5 * BLOCK, BLOCK)
    own = [lax.dynamic_slice_in_dim(t, core * HALF, HALF, 0) for t in tiles]
    sent = [lax.dynamic_slice_in_dim(t, (1 - core) * HALF, HALF, 0) for t in tiles]
    sent = [shift(t, "core", 1) for t in sent]
    panel_rows = place([own[0], sent[0], own[1], sent[1]], quad, 1)
    v = lax.select_n(away["x"], v[0], v1, shift(v2, "x", 2), v3)
    u = lax.select_n(away["y"], u[0], u1, shift(u2, "y", 2), u3)
    v, u = in_step(v, u)
    v, u = sends(quarters(v), "y"), sends(quarters(u), "x")
    v, u, s = in_step(lax.select_n(away["y"], *v), lax.select_n(away["x"], *u), s)
    v = jnp.where(holds, v, shift(v, "zl", 1))
    u = jnp.where(holds, u, shift(u, "zl", 1))
    gathered = lax.all_gather(jnp.concatenate([v, u], axis=1), ("y", "x"))

    s = lax.select_n(away["x"], *sends(quarters(s), "x"))
    s, panel_rows = in_step(s, panel_rows)
    s = lax.select_n(away["y"], *sends(quarters(s), "y"))
    s = jnp.where(holds, s, shift(s, "zl", 1))
    s = place(pieces(s, "y"), where["y"])
    mine = place(pieces(s, "x"), where["x"]).reshape(5, BLOCK, BLOCK)
    other = shift(mine, "core", 1)

    gathered, mine, other, panel_rows = in_step(gathered, mine, other, panel_rows)
    far_other, far, near_other, near = update(left_u, earlier_right_factors, gathered, sixteen)
    far = far + shift(far_other, "core", 1)
    near = near + shift(near_other, "core", 1)
    far, near, mine, other = in_step(far, panel_rows - near, mine, other)
    far = shift(far, "zh", 1)
    factor_rows, inverse = factor_and_inverse(mine, other, core)
    updated = near - far

    chosen = jnp.logical_and(lax.axis_index(ROW) == owner, slot == zh)

    def solved(z):
        inv = lax.dynamic_slice_in_dim(inverse, z * HALF, HALF, 0)
        fac = lax.dynamic_slice_in_dim(factor_rows, z * HALF, HALF, 1)
        return jnp.where(chosen, fac, dot(updated, inv, 1, 1, lax.Precision.HIGH))

    def column(value, c):
        return lax.dynamic_slice_in_dim(value, c * BLOCK, BLOCK, 1)

    out_far = solved(1 - zh)
    scale = jnp.maximum(jnp.max(jnp.abs(out_far), axis=1), 1e-30)
    sent = shift((out_far / scale[:, None]).astype(jnp.float16), "zh", 1)
    out_far = sent.astype(F32) * shift(scale, "zh", 1)[:, None]
    out_near = solved(zh)
    out = [column(out_near, core), shift(column(out_near, 1 - core), "core", 1)]
    out += [column(out_far, core), shift(column(out_far, 1 - core), "core", 1)]
    return place(out, quad)


def solution(mesh):
    split = Mesh(mesh.devices.reshape(2, 4, 4, 2, 2), ("zl", "y", "x", "zh", "core"))
    return jax.shard_map(
        local,
        mesh=split,
        in_specs=(P(ROW, COL), P(ROW, COL), P(ROW, COL), P()),
        out_specs=P(ROW, COL),
        check_vma=False,
    )
```
